128 devices in a mesh: slide: 8 (over x, core), tile: 16 (over y, z).
Axes of the slice: x: 4, y: 4, z: 4, core: 2. Of those that a mesh axis runs over, the one named last changes fastest.
Arguments:
- tiles: float32 [4096, 1536], P(('slide', 'tile')), may hold values from -6 to 6
- mlp_gain: float32 [1536], replicated, may hold values from 0.25 to 1.75
- mlp_bias: float32 [1536], replicated, may hold values from -0.5 to 0.5
- gate_weight: bfloat16 [1536, 4096], P(None, 'tile'), may hold values from -0.15625 to 0.15625
- up_weight: bfloat16 [1536, 4096], P(None, 'tile'), may hold values from -0.15625 to 0.15625
- down_weight: bfloat16 [4096, 1536], P('tile'), may hold values from -0.09375 to 0.09375
- layer_scale: float32 [1536], replicated, may hold values from 0.1 to 1
- final_gain: float32 [1536], replicated, may hold values from 0.25 to 1.75
- final_bias: float32 [1536], replicated, may hold values from -0.5 to 0.5
- patch_weight: bfloat16 [1536, 768], replicated, may hold values from -0.15625 to 0.15625
- patch_bias: float32 [768], replicated, may hold values from -0.5 to 0.5
- slide_gain: float32 [768], replicated, may hold values from 0.25 to 1.75
- slide_bias: float32 [768], replicated, may hold values from -0.5 to 0.5
- w_query: float32 [768, 768], replicated
- w_key: float32 [768, 768], replicated
- w_value: float32 [768, 768], replicated, may hold values from -0.21875 to 0.21875
- w_out: float32 [768, 768], replicated, may hold values from -0.21875 to 0.21875
- slide_lengths: int32 [16], replicated, may hold values from 1 to 512, as said below
- tile_slot: int32 [4096], P(('slide', 'tile')), may hold values from 0 to 8191, as said below
Outputs:
- slide_out: float32 [16, 512, 768], P('tile', 'slide')
The draws below stay inside these ranges and needn't reach their ends.
Inputs may be any that keep to these rules, and one draw needn't show every extreme that they name: `slide_lengths`: tile counts of the slides: they sum to 4096, the largest is exactly 512, and every slide has at least one tile. tile_slot[t] = s * 512 + p puts tile t at position p of slide s; slide s uses exactly the positions 0 to slide_lengths[s] - 1, each once. The tiles of one device fall at most 1 at a time into one block of 64 consecutive positions of a slide that starts at a multiple of 64; every draw reaches 1 for every device in some block that is filled.
All inputs are finite; a program needn't handle non-finite values.
Results may differ from the reference program's by a relative error of at most 0.027.
Values may be sent and summed in bfloat16 or wider, within the bound.
A program may use at most 128 MiB of HBM per device.

```python
import math
import jax
import jax.numpy as jnp
from jax import lax

D_TILE = 1536
FF_TILE = 4096
D_SLIDE = 768
HEADS = 16
HEAD_DIM = 48
TILE_DEV = 32
SEQ_DEV = 64
SPAN_ONE = 1024
SPAN_TWO = 2048
SPAN_THREE = 4096
TILES = 4096
N_SLIDE = 8
N_TILE = 16


def shared_projection(key):
    return jax.random.normal(key, (D_SLIDE, D_SLIDE), jnp.float32) * D_SLIDE ** (-0.5)


def draw_w_query(key, part):
    common = shared_projection(key)
    key = jax.random.fold_in(key, 11)
    own_part = jax.random.normal(key, (D_SLIDE, D_SLIDE), jnp.float32) * D_SLIDE ** (-0.5)
    return common * 0.6 + own_part


def draw_w_key(key, part):
    common = shared_projection(key)
    key = jax.random.fold_in(key, 12)
    own_part = jax.random.normal(key, (D_SLIDE, D_SLIDE), jnp.float32) * D_SLIDE ** (-0.5)
    return common * 0.6 + own_part


def slide_plan(key):
    key = jax.random.fold_in(key, 5)
    seq_total = SEQ_DEV * N_SLIDE
    needed = TILES - seq_total
    pick_key, weight_key = jax.random.split(key)
    largest = jax.random.randint(pick_key, (), 0, N_TILE)
    weights = jnp.left_shift(jnp.int32(1), jax.random.randint(weight_key, (N_TILE,), 3, 8))
    others = jnp.arange(N_TILE) != largest

    def occupied(factor):
        return jnp.where(others, jnp.clip(factor * weights // 128, 1, seq_total), 0)

    def bisect(step_index, bounds):
        lower, upper = bounds
        middle = (lower + upper) // 2
        within = jnp.sum(occupied(middle)) <= needed
        return (jnp.where(within, middle, lower), jnp.where(within, upper, middle))
    start_bounds = (jnp.int32(0), jnp.int32(16 * seq_total + 1))
    lower = lax.fori_loop(0, 32, bisect, start_bounds)[0]
    baseline = occupied(lower)
    leftover = needed - jnp.sum(baseline)
    growable = others & (baseline < seq_total)
    order_rank = jnp.cumsum(growable.astype(jnp.int32)) - 1
    extra = (growable & (order_rank < leftover)).astype(jnp.int32)
    return jnp.where(others, baseline + extra, seq_total).astype(jnp.int32)


def draw_slide_lengths(key, part):
    return slide_plan(key)


def draw_tile_slot(key, part):
    lengths = slide_plan(key)
    key = jax.random.fold_in(key, 7)
    seq_total = SEQ_DEV * N_SLIDE
    devices = N_SLIDE * N_TILE
    device_ids = jnp.arange(devices)
    block_of = device_ids // N_TILE
    slide_of = device_ids % N_TILE
    occupied = jnp.clip(lengths[slide_of] - block_of * SEQ_DEV, 0, SEQ_DEV)
    block_ends = jnp.cumsum(occupied)
    starts = block_ends - occupied
    ordinal = jnp.arange(TILES)
    owner_device = jnp.searchsorted(block_ends, ordinal, side='right')
    position = slide_of[owner_device] * seq_total + block_of[owner_device] * SEQ_DEV + ordinal - starts[owner_device]
    source = ordinal % devices
    order_rank = ordinal // devices
    shuffles = jax.vmap(lambda sub_key: jax.random.permutation(sub_key, TILE_DEV))(jax.random.split(key, devices))
    row_index = shuffles[source, order_rank]
    return jnp.zeros((TILES,), jnp.int32).at[source * TILE_DEV + row_index].set(position.astype(jnp.int32))


def levels(stream_key, extent, pieces, least, high):
    loudness, own = 1.0, jax.random.fold_in(stream_key, 6)
    for dim, shards_of in pieces:
        heights = jnp.exp(jax.random.uniform(jax.random.fold_in(own, dim), (shards_of,), jnp.float32, least / len(pieces), high / len(pieces)))
        loudness = loudness * jnp.repeat(heights, extent[dim] // shards_of).reshape([-1 if axis == dim else 1 for axis in range(len(extent))])
    return loudness


def noise(own_key, dims, scale, bound, cuts=(), kind=jnp.bfloat16):
    values = jax.random.normal(own_key, dims, jnp.float32) * scale
    if len(cuts) > 0:
        values = levels(own_key, dims, cuts, -0.22, 0.18) * values
    return jnp.clip(values, min=-bound, max=bound).astype(kind)


def setup_inputs(seed: int = 0) -> dict:
    key_list = jax.random.split(jax.random.key(seed), 20)
    return {
        "tiles": noise(key_list[0], (TILES, D_TILE), 1.0, 6.0, ((0, 128),), jnp.float32),
        "mlp_gain": jnp.clip(1.0 + 0.15 * jax.random.normal(key_list[1], (D_TILE,), jnp.float32), 0.25, 1.75),
        "mlp_bias": jnp.clip(jax.random.uniform(key_list[2], (D_TILE,), jnp.float32, -0.5, 0.5), -0.5, 0.5),
        "gate_weight": noise(key_list[3], (D_TILE, FF_TILE), D_TILE ** -0.5, 0.15625, ((1, 16),)),
        "up_weight": noise(key_list[4], (D_TILE, FF_TILE), D_TILE ** -0.5, 0.15625, ((1, 16),)),
        "down_weight": noise(key_list[5], (FF_TILE, D_TILE), FF_TILE ** -0.5, 0.09375, ((0, 16),)),
        "layer_scale": jnp.clip(jnp.exp(jax.random.uniform(key_list[6], (D_TILE,), jnp.float32, math.log(0.1), math.log(1.0))), 0.1, 1.0),
        "final_gain": jnp.clip(1.0 + 0.15 * jax.random.normal(key_list[7], (D_TILE,), jnp.float32), 0.25, 1.75),
        "final_bias": jnp.clip(jax.random.uniform(key_list[8], (D_TILE,), jnp.float32, -0.5, 0.5), -0.5, 0.5),
        "patch_weight": noise(key_list[9], (D_TILE, D_SLIDE), D_TILE ** -0.5, 0.15625),
        "patch_bias": jnp.clip(jax.random.uniform(key_list[10], (D_SLIDE,), jnp.float32, -0.5, 0.5), -0.5, 0.5),
        "slide_gain": jnp.clip(1.0 + 0.15 * jax.random.normal(key_list[11], (D_SLIDE,), jnp.float32), 0.25, 1.75),
        "slide_bias": jnp.clip(jax.random.uniform(key_list[12], (D_SLIDE,), jnp.float32, -0.5, 0.5), -0.5, 0.5),
        "w_query": draw_w_query(jax.random.fold_in(key_list[19], 71), 0),
        "w_key": draw_w_key(jax.random.fold_in(key_list[19], 71), 0),
        "w_value": noise(key_list[15], (D_SLIDE, D_SLIDE), D_SLIDE ** -0.5, 0.21875, (), jnp.float32),
        "w_out": noise(key_list[16], (D_SLIDE, D_SLIDE), D_SLIDE ** -0.5, 0.21875, (), jnp.float32),
        "slide_lengths": draw_slide_lengths(jax.random.fold_in(key_list[19], 71), 0),
        "tile_slot": draw_tile_slot(jax.random.fold_in(key_list[19], 71), 0),
    }


epsilon = 1e-06
masked_score = -1e+30
highest = lax.Precision.HIGHEST

def layer_norm(values, scale_vec, shift_vec):
    average = lax.optimization_barrier(jnp.mean(values, axis=-1, keepdims=True))
    centred = values - average
    variance = lax.optimization_barrier(jnp.mean(centred * centred, axis=-1, keepdims=True))
    return centred * lax.rsqrt(variance + epsilon) * scale_vec + shift_vec

def compress(values, dilation):
    length, heads, width = values.shape
    folded = values.reshape(length // dilation, dilation, heads // dilation, dilation, width)
    picked = jnp.diagonal(folded, axis1=1, axis2=3)
    return jnp.moveaxis(picked, 3, 2).reshape(length // dilation, heads, width)

def expand(values, dilation):
    length, heads, width = values.shape
    eye_mask = jnp.eye(dilation, dtype=values.dtype)
    spread = values.reshape(length, 1, heads // dilation, dilation, width) * eye_mask[None, :, None, :, None]
    return spread.reshape(length * dilation, heads, width)

def selected(length, heads, dilation):
    return jnp.arange(length)[:, None] % dilation == jnp.arange(heads)[None, :] % dilation

def segment_attention(queries, key_rows, value_rows, key_valid):
    factor = queries.shape[-1] ** (-0.5)
    scores = jnp.einsum('sqhe,skhe->shqk', queries, key_rows, precision=highest) * factor
    allowed = jnp.transpose(key_valid, (0, 2, 1))[:, :, None, :]
    scores = jnp.where(allowed, scores, masked_score)
    row_max = lax.optimization_barrier(jnp.max(scores, axis=-1, keepdims=True))
    weights = jnp.exp(scores - row_max)
    row_total = lax.optimization_barrier(jnp.sum(weights, axis=-1))
    mixed = jnp.einsum('shqk,skhe->sqhe', weights, value_rows, precision=highest)
    mixed = mixed / jnp.transpose(row_total, (0, 2, 1))[..., None]
    log_total = jnp.transpose(row_max[..., 0] + jnp.log(row_total), (0, 2, 1))
    return (mixed, log_total)

def combine(branch_outs):
    best_log = None
    for mixed_full, log_full, chosen in branch_outs:
        candidate = jnp.where(chosen, log_full, masked_score)
        best_log = candidate if best_log is None else jnp.maximum(best_log, candidate)
    numerator = 0.0
    denominator = 0.0
    for mixed_full, log_full, chosen in branch_outs:
        candidate = jnp.where(chosen, log_full, masked_score)
        weight = jnp.where(chosen, jnp.exp(candidate - best_log), 0.0)
        numerator = numerator + weight[..., None] * mixed_full
        denominator = denominator + weight
    return numerator / denominator[..., None]

def reference(tiles, mlp_gain, mlp_bias, gate_weight, up_weight, down_weight, layer_scale, final_gain, final_bias, patch_weight, patch_bias, slide_gain, slide_bias, w_query, w_key, w_value, w_out, slide_lengths, tile_slot):
    normed = layer_norm(tiles, mlp_gain, mlp_bias).astype(jnp.bfloat16)
    gate_out = jnp.dot(normed, gate_weight, preferred_element_type=jnp.float32)
    up_out = jnp.dot(normed, up_weight, preferred_element_type=jnp.float32)
    hidden = (jax.nn.silu(gate_out) * up_out).astype(jnp.bfloat16)
    group_width = FF_TILE // N_TILE

    def add_group(running, group_id):
        first_unit = (group_id * group_width).astype(jnp.int32)
        hidden_part = lax.dynamic_slice_in_dim(hidden, first_unit, group_width, 1)
        down_part = lax.dynamic_slice_in_dim(down_weight, first_unit, group_width, 0)
        term = jnp.dot(hidden_part, down_part, preferred_element_type=jnp.float32).astype(jnp.bfloat16)
        term = lax.optimization_barrier(term)
        return (running + term.astype(jnp.float32), None)
    mixed = lax.scan(add_group, jnp.zeros(tiles.shape, jnp.float32), jnp.arange(N_TILE, dtype=jnp.int32))[0]
    final = layer_norm(tiles + layer_scale * mixed, final_gain, final_bias).astype(jnp.bfloat16)
    embed = jnp.dot(final, patch_weight, preferred_element_type=jnp.float32) + patch_bias
    seq_total = SEQ_DEV * N_SLIDE
    canvas = jnp.zeros((N_TILE * seq_total, D_SLIDE), jnp.float32).at[tile_slot].set(embed)
    canvas = canvas.reshape(N_TILE, seq_total, D_SLIDE)
    spans = ((min(SPAN_ONE, seq_total), 1), (min(SPAN_TWO, seq_total), 2), (min(SPAN_THREE, seq_total), 4))

    def one_slide(inputs):
        stream, length = inputs
        valid = jnp.arange(seq_total) < length
        normed_slide = layer_norm(stream, slide_gain, slide_bias)
        queries = jnp.dot(normed_slide, w_query, precision=highest).reshape(seq_total, HEADS, HEAD_DIM)
        keys = jnp.dot(normed_slide, w_key, precision=highest).reshape(seq_total, HEADS, HEAD_DIM)
        values = jnp.dot(normed_slide, w_value, precision=highest).reshape(seq_total, HEADS, HEAD_DIM)
        key_valid = jnp.broadcast_to(valid[:, None, None], (seq_total, HEADS, 1))
        branch_outs = []
        for seg_span, dilation in spans:
            segments = seq_total // seg_span
            query_rows = compress(queries, dilation).reshape(segments, -1, HEADS, HEAD_DIM)
            key_rows = compress(keys, dilation).reshape(segments, -1, HEADS, HEAD_DIM)
            value_rows = compress(values, dilation).reshape(segments, -1, HEADS, HEAD_DIM)
            valid_rows = compress(key_valid, dilation)[:, :, 0].reshape(segments, -1, HEADS)
            mixed_rows, log_rows = segment_attention(query_rows, key_rows, value_rows, valid_rows)
            mixed_full = expand(mixed_rows.reshape(-1, HEADS, HEAD_DIM), dilation)
            log_full = expand(log_rows.reshape(-1, HEADS, 1), dilation)[:, :, 0]
            branch_outs.append((mixed_full, log_full, selected(seq_total, HEADS, dilation)))
        attention = combine(branch_outs).reshape(seq_total, D_SLIDE)
        result = stream + jnp.dot(attention, w_out, precision=highest)
        return jnp.where(valid[:, None], result, 0.0)
    return lax.map(one_slide, (canvas, slide_lengths))
```

```python
import jax
import jax.numpy as jnp
from jax import lax
from jax.experimental import pallas as pl
from jax.experimental.pallas import tpu as pltpu
from jax.sharding import PartitionSpec as P

D_TILE = 1536
D_SLIDE = 768
HEADS = 16
HEAD_DIM = 48
TILE_DEV = 32
SEQ_DEV = 64
SEQ = 512
GROUP = 256
MESH = pl.DeviceIdType.MESH
F32 = jnp.float32
BF16 = jnp.bfloat16
epsilon = 1e-06
masked_score = -1e30


def layer_norm(values, scale_vec, shift_vec):
    average = jnp.mean(values, axis=-1, keepdims=True)
    centred = values - average
    variance = jnp.mean(centred * centred, axis=-1, keepdims=True)
    return centred * lax.rsqrt(variance + epsilon) * scale_vec + shift_vec


def iota(shape, dim):
    return lax.broadcasted_iota(jnp.int32, shape, dim)


def offset_of(i):
    return i + (i // 2) * (1 - 2 * (i % 2))


def kernel(
    tiles_h, mlp_gain_h, mlp_bias_h, gate_h, up_h, down_h, layer_scale_h, final_gain_h, final_bias_h,
    patch_h, patch_bias_h, slide_gain_h, slide_bias_h, wq_h, wk_h, wv_h, wo_h, lengths, slot_h,
    out,
    tiles, mlp_gain, mlp_bias, gate, up, down, layer_scale, final_gain, final_bias,
    patch, patch_bias, slide_gain, slide_bias, wq, wk, wv, wo, slot,
    rows, part, got1, fold, got2, wkv16, wq16, wo16,
    pos_out, pos_in, pos_all, send_slots, got_slots, slots, one_hot, canvas, normed_all, kv, mult, att,
    load_sem, ag1_s, ag2_s, ag_r, rs1_s, rs1_r, rs2_s, rs2_r,
    pos_s, pos_r, pa_s, pa_r, sl_s, sl_r, dg_s, dg_r,
):
    s = lax.axis_index("slide")
    t = lax.axis_index("tile")
    x, c = s // 2, s % 2
    y, z = t // 4, t % 4

    def first(k):
        return (s, ((y + c * k) % 4) * 4 + (z + (1 - c) * k) % 4)

    def second(k):
        return (s, ((y + (1 - c) * k) % 4) * 4 + (z + c * k) % 4)

    def on_tile(k):
        return (s, (t + k) % 16)

    def on_slide(dx, dc):
        return (((x + dx) % 4) * 2 + (c + dc) % 2, t)

    def remote(src, dst, send_sem, recv_sem, device):
        return pltpu.make_async_remote_copy(
            src_ref=src, dst_ref=dst, send_sem=send_sem, recv_sem=recv_sem,
            device_id=device, device_id_type=MESH,
        )

    pairs = (
        (tiles_h, tiles), (mlp_gain_h, mlp_gain), (mlp_bias_h, mlp_bias), (slot_h, slot),
        (gate_h, gate), (up_h, up), (down_h, down), (layer_scale_h, layer_scale),
        (final_gain_h, final_gain), (final_bias_h, final_bias), (patch_h, patch), (patch_bias_h, patch_bias),
        (wk_h, wk), (wv_h, wv), (wq_h, wq), (wo_h, wo), (slide_gain_h, slide_gain), (slide_bias_h, slide_bias),
    )
    loads = [pltpu.make_async_copy(a, b, load_sem.at[i]) for i, (a, b) in enumerate(pairs)]
    for load in loads:
        load.start()

    barrier = pltpu.get_barrier_semaphore()

    def greet(k, carry):
        pl.semaphore_signal(barrier, inc=1, device_id=on_tile(k), device_id_type=MESH)
        return carry

    lax.fori_loop(1, 16, greet, 0)

    def greet_slide(k, carry):
        pl.semaphore_signal(barrier, inc=1, device_id=on_slide(k // 2, k % 2), device_id_type=MESH)
        return carry

    lax.fori_loop(1, 8, greet_slide, 0)

    for i in range(3):
        loads[i].wait()
    rows[0] = layer_norm(tiles[...], mlp_gain[...], mlp_bias[...]).astype(BF16)

    pl.semaphore_wait(barrier, 22)

    def ag1(j):
        return remote(rows.at[0], rows.at[j], ag1_s.at[j], ag_r.at[j], first(offset_of(j)))

    for j in range(1, 4):
        ag1(j).start()

    def ag2(i, j):
        return remote(
            rows.at[j], rows.at[i * 4 + j], ag2_s.at[i * 4 + j], ag_r.at[i * 4 + j], second(offset_of(i))
        )

    for i in range(1, 4):
        ag2(i, 0).start()

    loads[3].wait()
    spot = slot[...]
    row_id = iota((128, TILE_DEV), 0)
    match = (spot // 512 == row_id // 8) & ((spot // 64) % 8 == row_id % 8)
    place = jnp.sum(jnp.where(match, (spot % 512 + 1).astype(F32), 0.0), axis=1, keepdims=True)
    pos_out[...] = jnp.broadcast_to(place, (128, 128)).reshape(16, 8, 128)
    pos_in[0] = pos_out[t]

    def pos_copy(k):
        return remote(pos_out.at[(t + k) % 16], pos_in.at[k], pos_s.at[k], pos_r.at[k], on_tile(k))

    def pos_start(k, carry):
        pos_copy(k).start()
        return carry

    lax.fori_loop(1, 16, pos_start, 0)

    for j in range(1, 4):
        ag1(j).wait_recv()
        for i in range(1, 4):
            ag2(i, j).start()

    def pos_wait(k, carry):
        pos_copy(k).wait_recv()
        return carry

    lax.fori_loop(1, 16, pos_wait, 0)
    turned = jnp.transpose(pos_in[...].reshape(128, 128))
    pos_all[0] = turned[0:8]

    def pa_copy(k):
        return remote(pos_all.at[0], pos_all.at[k], pa_s.at[k], pa_r.at[k], on_slide(k // 2, k % 2))

    def pa_start(k, carry):
        pa_copy(k).start()
        return carry

    lax.fori_loop(1, 8, pa_start, 0)

    for i in range(4, 7):
        loads[i].wait()

    def rs1(i):
        return remote(
            part.at[pl.ds(4 * i, 4)], got1.at[i - 1], rs1_s.at[i], rs1_r.at[i], second(4 - offset_of(i))
        )

    def batch(i, carry):
        @pl.when(i > 0)
        def _():
            for j in range(4):
                ag2(i, j).wait_recv()

        block = rows[pl.ds(4 * i, 4)].reshape(128, D_TILE)
        gate_out = jnp.dot(block, gate[...], preferred_element_type=F32)
        up_out = jnp.dot(block, up[...], preferred_element_type=F32)
        hidden = (gate_out / (1.0 + jnp.exp(-gate_out)) * up_out).astype(BF16)
        part[pl.ds(4 * i, 4)] = (
            jnp.dot(hidden, down[...], preferred_element_type=F32).astype(BF16).reshape(4, TILE_DEV, D_TILE)
        )

        @pl.when(i > 0)
        def _():
            rs1(i).start()

        return carry

    lax.fori_loop(0, 4, batch, 0)

    for i in range(12, 16):
        loads[i].wait()

    def convert(k, carry):
        at = pl.ds(pl.multiple_of(k * 128, 128), 128)
        wkv16[at, 0:D_SLIDE] = wk[at, :].astype(BF16)
        wkv16[at, D_SLIDE : 2 * D_SLIDE] = wv[at, :].astype(BF16)
        wq16[at, :] = wq[at, :].astype(BF16)
        wo16[at, :] = wo[at, :].astype(BF16)
        return carry

    lax.fori_loop(0, 6, convert, 0)

    def pa_wait(k, carry):
        pa_copy(k).wait_recv()
        return carry

    lax.fori_loop(1, 8, pa_wait, 0)
    position = (iota((SEQ, 128), 0) + 1).astype(F32)
    for k in range(8):
        one_hot[:, k * 128 : (k + 1) * 128] = jnp.where(position == pos_all[k][0:1], 1.0, 0.0).astype(BF16)

    length = lengths[t]
    row = iota((256, SEQ), 0)
    key = iota((256, SEQ), 1)
    head, query = row // 64, row % 64
    weight = (
        1.0
        + jnp.where((query % 2 == head % 2) & (key % 2 == head % 2), 1.0, 0.0)
        + jnp.where((query % 4 == head) & (key % 4 == head), 1.0, 0.0)
    )
    mult[...] = jnp.where(key < length, weight, 0.0)

    for i in range(1, 4):
        rs1(i).wait_recv()

    def rs2(j):
        return remote(fold.at[j - 1], got2.at[j - 1], rs2_s.at[j], rs2_r.at[j], first(4 - offset_of(j)))

    def line_sum(j):
        return (
            part[j].astype(F32) + got1[0, j].astype(F32) + got1[1, j].astype(F32) + got1[2, j].astype(F32)
        )

    for j in range(1, 4):
        fold[j - 1] = line_sum(j).astype(BF16)
        rs2(j).start()
    mixed = line_sum(0)
    for i in range(7, 12):
        loads[i].wait()
    for j in range(1, 4):
        rs2(j).wait_recv()
    mixed = mixed + got2[0].astype(F32) + got2[1].astype(F32) + got2[2].astype(F32)
    final = layer_norm(tiles[...] + layer_scale[...] * mixed, final_gain[...], final_bias[...]).astype(BF16)
    embed = (jnp.dot(final, patch[...], preferred_element_type=F32) + patch_bias[...]).astype(BF16)

    slot_id = iota((256, TILE_DEV), 0)
    hit = (spot // 512 == slot_id // 16) & ((spot // 64) % 8 == slot_id % 8)
    left = jnp.where(hit & (slot_id % 16 < 8), 1.0, 0.0).astype(BF16)
    right = jnp.where(hit & (slot_id % 16 >= 8), 1.0, 0.0).astype(BF16)
    send_slots[...] = (
        (
            jnp.dot(left, embed[:, 0:384], preferred_element_type=F32)
            + jnp.dot(right, embed[:, 384:768], preferred_element_type=F32)
        )
        .astype(BF16)
        .reshape(16, 16, 384)
    )

    def slot_copy(k):
        return remote(send_slots.at[(t + k) % 16], got_slots.at[k], sl_s.at[k], sl_r.at[k], on_tile(k))

    def slot_start(k, carry):
        slot_copy(k).start()
        return carry

    lax.fori_loop(1, 16, slot_start, 0)
    got_slots[0] = send_slots[t]

    def slot_wait(k, carry):
        slot_copy(k).wait_recv()
        return carry

    lax.fori_loop(1, 16, slot_wait, 0)
    wide = got_slots[...].astype(F32)
    slots[0, :, 0:384] = wide[:, 0:8, :].reshape(128, 384).astype(BF16)
    slots[0, :, 384:768] = wide[:, 8:16, :].reshape(128, 384).astype(BF16)

    def far(i):
        k = 2 * offset_of(i)
        return remote(slots.at[0], slots.at[k], dg_s.at[k], dg_r.at[k], on_slide(offset_of(i), 0))

    def near(i):
        k = 2 * offset_of(i)
        return remote(slots.at[k], slots.at[k + 1], dg_s.at[k + 1], dg_r.at[k + 1], on_slide(0, 1))

    for i in range(1, 4):
        far(i).start()
    near(0).start()

    def place_pair(i):
        k = 2 * offset_of(i)
        return jnp.dot(
            one_hot[:, k * 128 : (k + 2) * 128], slots[k : k + 2].reshape(256, D_SLIDE), preferred_element_type=F32
        )

    near(0).wait_recv()
    canvas[...] = place_pair(0)
    for i in range(1, 4):
        far(i).wait_recv()
        near(i).start()
    for i in range(1, 4):
        near(i).wait_recv()
        canvas[...] += place_pair(i)
    for i in range(16, 18):
        loads[i].wait()
    normed_all[...] = layer_norm(canvas[...], slide_gain[...], slide_bias[...]).astype(BF16)
    mine = pl.ds(pl.multiple_of(s * SEQ_DEV, SEQ_DEV), SEQ_DEV)
    kv[...] = jnp.dot(normed_all[...], wkv16[...], preferred_element_type=F32).astype(BF16)
    queries = jnp.dot(normed_all[mine, :], wq16[...], preferred_element_type=F32) * HEAD_DIM ** (-0.5)

    head_row = iota((256, 256), 0) // 64
    lane = iota((256, 256), 1)
    att[...] = jnp.zeros_like(att)
    for w, start in enumerate((0, 128, 384, 512)):
        low = (4 * w + head_row) * HEAD_DIM - start
        own = (lane >= low) & (lane < low + HEAD_DIM)
        window = queries[:, start : start + 256]
        stacked = jnp.where(own, jnp.concatenate([window] * 4, axis=0), 0.0).astype(BF16)
        scores = lax.dot_general(
            stacked, kv[:, start : start + 256], (((1,), (1,)), ((), ())), preferred_element_type=F32
        )
        counted = mult[...]
        scores = jnp.where(counted > 0.0, scores, masked_score)
        weights = jnp.exp(scores - jnp.max(scores, axis=1, keepdims=True)) * counted
        total = jnp.sum(weights, axis=1, keepdims=True)
        mixed_rows = jnp.dot(
            weights.astype(BF16), kv[:, D_SLIDE + start : D_SLIDE + start + 256], preferred_element_type=F32
        )
        mixed_rows = jnp.where(own, mixed_rows / total, 0.0)
        att[:, start : start + 256] += (
            mixed_rows[0:64] + mixed_rows[64:128] + mixed_rows[128:192] + mixed_rows[192:256]
        )
    result = canvas[mine, :] + jnp.dot(att[...].astype(BF16), wo16[...], preferred_element_type=F32)
    here = iota((SEQ_DEV, D_SLIDE), 0) + s * SEQ_DEV
    out[0] = jnp.where(here < length, result, 0.0)

    for j in range(1, 4):
        ag1(j).wait_send()
        rs1(j).wait_send()
        rs2(j).wait_send()
        far(j).wait_send()
        for i in range(0, 4):
            ag2(j, i).wait_send()
    for i in range(4):
        near(i).wait_send()

    def sent(k, carry):
        pos_copy(k).wait_send()
        slot_copy(k).wait_send()
        return carry

    lax.fori_loop(1, 16, sent, 0)

    def sent_pa(k, carry):
        pa_copy(k).wait_send()
        return carry

    lax.fori_loop(1, 8, sent_pa, 0)


def per_device(
    tiles, mlp_gain, mlp_bias, gate_weight, up_weight, down_weight, layer_scale, final_gain, final_bias,
    patch_weight, patch_bias, slide_gain, slide_bias, w_query, w_key, w_value, w_out, slide_lengths, tile_slot,
):
    wide = lambda v: v.reshape(1, -1)
    hbm = pl.BlockSpec(memory_space=pl.ANY)
    dma = pltpu.SemaphoreType.DMA
    vm = pltpu.VMEM
    return pl.pallas_call(
        kernel,
        out_shape=jax.ShapeDtypeStruct((1, SEQ_DEV, D_SLIDE), F32),
        in_specs=[hbm] * 17 + [pl.BlockSpec(memory_space=pltpu.SMEM)] + [hbm],
        out_specs=pl.BlockSpec(memory_space=pltpu.VMEM),
        scratch_shapes=[
            vm((TILE_DEV, D_TILE), F32), vm((1, D_TILE), F32), vm((1, D_TILE), F32),
            vm((D_TILE, GROUP), BF16), vm((D_TILE, GROUP), BF16), vm((GROUP, D_TILE), BF16),
            vm((1, D_TILE), F32), vm((1, D_TILE), F32), vm((1, D_TILE), F32),
            vm((D_TILE, D_SLIDE), BF16), vm((1, D_SLIDE), F32), vm((1, D_SLIDE), F32), vm((1, D_SLIDE), F32),
            vm((D_SLIDE, D_SLIDE), F32), vm((D_SLIDE, D_SLIDE), F32),
            vm((D_SLIDE, D_SLIDE), F32), vm((D_SLIDE, D_SLIDE), F32),
            vm((1, TILE_DEV), jnp.int32),
            vm((16, TILE_DEV, D_TILE), BF16), vm((16, TILE_DEV, D_TILE), BF16),
            vm((3, 4, TILE_DEV, D_TILE), BF16), vm((3, TILE_DEV, D_TILE), BF16), vm((3, TILE_DEV, D_TILE), BF16),
            vm((D_SLIDE, 2 * D_SLIDE), BF16), vm((D_SLIDE, D_SLIDE), BF16), vm((D_SLIDE, D_SLIDE), BF16),
            vm((16, 8, 128), F32), vm((16, 8, 128), F32), vm((8, 8, 128), F32),
            vm((16, 16, 384), BF16), vm((16, 16, 384), BF16), vm((8, 128, D_SLIDE), BF16),
            vm((SEQ, 1024), BF16), vm((SEQ, D_SLIDE), F32), vm((SEQ, D_SLIDE), BF16),
            vm((SEQ, 2 * D_SLIDE), BF16), vm((256, SEQ), F32), vm((SEQ_DEV, D_SLIDE), F32),
            dma((18,)), dma((4,)), dma((16,)), dma((16,)), dma((4,)), dma((4,)), dma((4,)), dma((4,)),
            dma((16,)), dma((16,)), dma((8,)), dma((8,)), dma((16,)), dma((16,)), dma((8,)), dma((8,)),
        ],
        compiler_params=pltpu.CompilerParams(
            collective_id=0, has_side_effects=True, vmem_limit_bytes=56 * 2**20
        ),
        name="slide_kernel",
    )(
        tiles, wide(mlp_gain), wide(mlp_bias), gate_weight, up_weight, down_weight, wide(layer_scale),
        wide(final_gain), wide(final_bias), patch_weight, wide(patch_bias), wide(slide_gain), wide(slide_bias),
        w_query, w_key, w_value, w_out, slide_lengths, wide(tile_slot),
    )


def solution(mesh):
    both = P(("slide", "tile"))
    placed = (
        P(("slide", "tile"), None), P(), P(), P(None, "tile"), P(None, "tile"), P("tile", None),
        P(), P(), P(), P(), P(), P(), P(), P(), P(), P(), P(), P(), both,
    )
    return jax.shard_map(
        per_device, mesh=mesh, in_specs=placed, out_specs=P("tile", "slide", None), check_vma=False
    )
```

```python
import jax
import jax.numpy as jnp
from jax import lax
from jax.experimental import pallas as pl
from jax.experimental.pallas import tpu as pltpu
from jax.sharding import PartitionSpec as P

D_TILE = 1536
D_SLIDE = 768
HEADS = 16
HEAD_DIM = 48
TILE_DEV = 32
SEQ_DEV = 64
SEQ = 512
GROUP = 256
MESH = pl.DeviceIdType.MESH
F32 = jnp.float32
BF16 = jnp.bfloat16
epsilon = 1e-06
masked_score = -1e30


def layer_norm(values, scale_vec, shift_vec):
    average = jnp.mean(values, axis=-1, keepdims=True)
    centred = values - average
    variance = jnp.mean(centred * centred, axis=-1, keepdims=True)
    return centred * lax.rsqrt(variance + epsilon) * scale_vec + shift_vec


def iota(shape, dim):
    return lax.broadcasted_iota(jnp.int32, shape, dim)


def offset_of(i):
    return i + (i // 2) * (1 - 2 * (i % 2))


def kernel(
    tiles_h, mlp_gain_h, mlp_bias_h, gate_h, up_h, down_h, layer_scale_h, final_gain_h, final_bias_h,
    patch_h, patch_bias_h, slide_gain_h, slide_bias_h, wq_h, wk_h, wv_h, wo_h, lengths, slot_h,
    out,
    tiles, mlp_gain, mlp_bias, gate, up, down, layer_scale, final_gain, final_bias,
    patch, patch_bias, slide_gain, slide_bias, wq, wk, wv, wo, slot,
    rows, part, got1, fold, got2, wkv16, wq16, wo16,
    pos_out, pos_in, pos_all, send_slots, got_slots, slots, one_hot, canvas, normed_all, kv, mult, att,
    load_sem, ag1_s, ag2_s, ag_r, rs1_s, rs1_r, rs2_s, rs2_r,
    pos_s, pos_r, pa_s, pa_r, sl_s, sl_r, dg_s, dg_r,
):
    s = lax.axis_index("slide")
    t = lax.axis_index("tile")
    x, c = s // 2, s % 2
    y, z = t // 4, t % 4

    def first(k):
        return (s, ((y + c * k) % 4) * 4 + (z + (1 - c) * k) % 4)

    def second(k):
        return (s, ((y + (1 - c) * k) % 4) * 4 + (z + c * k) % 4)

    def on_tile(k):
        return (s, (t + k) % 16)

    def on_slide(dx, dc):
        return (((x + dx) % 4) * 2 + (c + dc) % 2, t)

    def remote(src, dst, send_sem, recv_sem, device):
        return pltpu.make_async_remote_copy(
            src_ref=src, dst_ref=dst, send_sem=send_sem, recv_sem=recv_sem,
            device_id=device, device_id_type=MESH,
        )

    pending = []

    def sent(copy, first_k, last_k):
        def one(k, carry):
            copy(k).wait_send()
            return carry

        pending.append(lambda: lax.fori_loop(first_k, last_k, one, 0))

    barrier = pltpu.get_barrier_semaphore()

    def greet(device):
        pl.semaphore_signal(barrier, inc=1, device_id=device, device_id_type=MESH)

    for k in range(1, 4):
        greet(first(k))
        greet(second(k))
    for k in range(1, 8):
        greet(on_slide(k // 2, k % 2))

    pairs = (
        (tiles_h, tiles), (mlp_gain_h, mlp_gain), (mlp_bias_h, mlp_bias),
        (gate_h, gate), (up_h, up), (down_h, down), (slot_h, slot), (layer_scale_h, layer_scale),
        (final_gain_h, final_gain), (final_bias_h, final_bias), (patch_h, patch), (patch_bias_h, patch_bias),
        (wk_h, wk), (wv_h, wv), (wq_h, wq), (wo_h, wo), (slide_gain_h, slide_gain), (slide_bias_h, slide_bias),
    )
    loads = [pltpu.make_async_copy(a, b, load_sem.at[i]) for i, (a, b) in enumerate(pairs)]
    for load in loads:
        load.start()
    for i in range(3):
        loads[i].wait()
    rows[0] = layer_norm(tiles[...], mlp_gain[...], mlp_bias[...]).astype(BF16)

    pl.semaphore_wait(barrier, 13)

    def ag1(j):
        return remote(rows.at[0], rows.at[4 * j], ag1_s.at[j], ag_r.at[4 * j], first(offset_of(j)))

    for j in range(1, 4):
        ag1(j).start()
        pending.append(ag1(j).wait_send)

    def ag2(i, j):
        return remote(
            rows.at[4 * j], rows.at[4 * j + i], ag2_s.at[4 * j + i], ag_r.at[4 * j + i], second(offset_of(i))
        )

    for i in range(1, 4):
        ag2(i, 0).start()
        pending.append(ag2(i, 0).wait_send)
    for j in range(1, 4):
        ag1(j).wait_recv()
        for i in range(1, 4):
            ag2(i, j).start()
            pending.append(ag2(i, j).wait_send)
    for i in range(3, 6):
        loads[i].wait()

    def rs1(i, j):
        return remote(
            part.at[4 * j + i], got1.at[j, i - 1], rs1_s.at[4 * j + i], rs1_r.at[4 * j + i], second(4 - offset_of(i))
        )

    def batch(j, carry):
        for i in range(1, 4):
            ag2(i, j).wait_recv()
        block = rows[pl.ds(4 * j, 4)].reshape(128, D_TILE)
        gate_out = jnp.dot(block, gate[...], preferred_element_type=F32)
        up_out = jnp.dot(block, up[...], preferred_element_type=F32)
        hidden = (gate_out / (1.0 + jnp.exp(-gate_out)) * up_out).astype(BF16)
        part[pl.ds(4 * j, 4)] = (
            jnp.dot(hidden, down[...], preferred_element_type=F32).astype(BF16).reshape(4, TILE_DEV, D_TILE)
        )
        for i in range(1, 4):
            rs1(i, j).start()
        return carry

    lax.fori_loop(0, 4, batch, 0)
    for j in range(4):
        for i in range(1, 4):
            pending.append(rs1(i, j).wait_send)

    loads[6].wait()
    spot = slot[...]
    row_id = iota((128, TILE_DEV), 0)
    match = (spot // 512 == row_id // 8) & ((spot // 64) % 8 == row_id % 8)
    place = jnp.sum(jnp.where(match, (spot % 512 + 1).astype(F32), 0.0), axis=1, keepdims=True)
    pos_out[...] = jnp.broadcast_to(place, (128, 128)).reshape(16, 8, 128)
    pos_in[0] = pos_out[t]

    def pos_copy(k):
        return remote(pos_out.at[(t + k) % 16], pos_in.at[k], pos_s.at[k], pos_r.at[k], on_tile(k))

    def pos_start(k, carry):
        pos_copy(k).start()
        return carry

    lax.fori_loop(1, 16, pos_start, 0)
    sent(pos_copy, 1, 16)

    for i in range(12, 16):
        loads[i].wait()

    def convert(k, carry):
        at = pl.ds(pl.multiple_of(k * 128, 128), 128)
        wkv16[at, 0:D_SLIDE] = wk[at, :].astype(BF16)
        wkv16[at, D_SLIDE : 2 * D_SLIDE] = wv[at, :].astype(BF16)
        wq16[at, :] = wq[at, :].astype(BF16)
        wo16[at, :] = wo[at, :].astype(BF16)
        return carry

    lax.fori_loop(0, 6, convert, 0)

    length = lengths[t]
    row = iota((256, SEQ), 0)
    key = iota((256, SEQ), 1)
    head, query = row // 64, row % 64
    weight = (
        1.0
        + jnp.where((query % 2 == head % 2) & (key % 2 == head % 2), 1.0, 0.0)
        + jnp.where((query % 4 == head) & (key % 4 == head), 1.0, 0.0)
    )
    mult[...] = jnp.where(key < length, weight, 0.0)

    def rs2(j):
        return remote(fold.at[j - 1], got2.at[j - 1], rs2_s.at[j], rs2_r.at[j], first(4 - offset_of(j)))

    def line_sum(j):
        for i in range(1, 4):
            rs1(i, j).wait_recv()
        return (
            part[4 * j].astype(F32) + got1[j, 0].astype(F32) + got1[j, 1].astype(F32) + got1[j, 2].astype(F32)
        )

    for j in range(1, 4):
        fold[j - 1] = line_sum(j).astype(BF16)
        rs2(j).start()
        pending.append(rs2(j).wait_send)
    mixed = line_sum(0)

    def pos_wait(k, carry):
        pos_copy(k).wait_recv()
        return carry

    lax.fori_loop(1, 16, pos_wait, 0)
    turned = jnp.transpose(pos_in[...].reshape(128, 128))
    pos_all[0] = turned[0:8]

    def pa_copy(k):
        return remote(pos_all.at[0], pos_all.at[k], pa_s.at[k], pa_r.at[k], on_slide(k // 2, k % 2))

    def pa_start(k, carry):
        pa_copy(k).start()
        return carry

    lax.fori_loop(1, 8, pa_start, 0)
    sent(pa_copy, 1, 8)

    for i in range(7, 12):
        loads[i].wait()
    for j in range(1, 4):
        rs2(j).wait_recv()
    mixed = mixed + got2[0].astype(F32) + got2[1].astype(F32) + got2[2].astype(F32)
    final = layer_norm(tiles[...] + layer_scale[...] * mixed, final_gain[...], final_bias[...]).astype(BF16)
    embed = (jnp.dot(final, patch[...], preferred_element_type=F32) + patch_bias[...]).astype(BF16)

    slot_id = iota((256, TILE_DEV), 0)
    hit = (spot // 512 == slot_id // 16) & ((spot // 64) % 8 == slot_id % 8)
    left = jnp.where(hit & (slot_id % 16 < 8), 1.0, 0.0).astype(BF16)
    right = jnp.where(hit & (slot_id % 16 >= 8), 1.0, 0.0).astype(BF16)
    send_slots[...] = (
        (
            jnp.dot(left, embed[:, 0:384], preferred_element_type=F32)
            + jnp.dot(right, embed[:, 384:768], preferred_element_type=F32)
        )
        .astype(BF16)
        .reshape(16, 16, 384)
    )

    def slot_copy(k):
        return remote(send_slots.at[(t + k) % 16], got_slots.at[k], sl_s.at[k], sl_r.at[k], on_tile(k))

    def slot_start(k, carry):
        slot_copy(k).start()
        return carry

    lax.fori_loop(1, 16, slot_start, 0)
    sent(slot_copy, 1, 16)
    got_slots[0] = send_slots[t]

    def pa_wait(k, carry):
        pa_copy(k).wait_recv()
        return carry

    lax.fori_loop(1, 8, pa_wait, 0)
    position = (iota((SEQ, 128), 0) + 1).astype(F32)
    for k in range(8):
        one_hot[:, k * 128 : (k + 1) * 128] = jnp.where(position == pos_all[k][0:1], 1.0, 0.0).astype(BF16)

    def slot_wait(k, carry):
        slot_copy(k).wait_recv()
        return carry

    lax.fori_loop(1, 16, slot_wait, 0)
    wide = got_slots[...].astype(F32)
    slots[0, :, 0:384] = wide[:, 0:8, :].reshape(128, 384).astype(BF16)
    slots[0, :, 384:768] = wide[:, 8:16, :].reshape(128, 384).astype(BF16)

    def far(i):
        k = 2 * offset_of(i)
        return remote(slots.at[0], slots.at[k], dg_s.at[k], dg_r.at[k], on_slide(offset_of(i), 0))

    def near(i):
        k = 2 * offset_of(i)
        return remote(slots.at[k], slots.at[k + 1], dg_s.at[k + 1], dg_r.at[k + 1], on_slide(0, 1))

    for i in range(1, 4):
        far(i).start()
        pending.append(far(i).wait_send)
    near(0).start()
    pending.append(near(0).wait_send)

    def place_pair(i):
        k = 2 * offset_of(i)
        return jnp.dot(
            one_hot[:, k * 128 : (k + 2) * 128], slots[k : k + 2].reshape(256, D_SLIDE), preferred_element_type=F32
        )

    near(0).wait_recv()
    canvas[...] = place_pair(0)
    for i in range(1, 4):
        far(i).wait_recv()
        near(i).start()
        pending.append(near(i).wait_send)
    for i in range(1, 4):
        near(i).wait_recv()
        canvas[...] += place_pair(i)
    for i in range(16, 18):
        loads[i].wait()
    normed_all[...] = layer_norm(canvas[...], slide_gain[...], slide_bias[...]).astype(BF16)
    mine = pl.ds(pl.multiple_of(s * SEQ_DEV, SEQ_DEV), SEQ_DEV)
    kv[...] = jnp.dot(normed_all[...], wkv16[...], preferred_element_type=F32).astype(BF16)
    queries = jnp.dot(normed_all[mine, :], wq16[...], preferred_element_type=F32) * HEAD_DIM ** (-0.5)

    head_row = iota((256, 256), 0) // 64
    lane = iota((256, 256), 1)
    att[...] = jnp.zeros_like(att)
    for w, start in enumerate((0, 128, 384, 512)):
        low = (4 * w + head_row) * HEAD_DIM - start
        own = (lane >= low) & (lane < low + HEAD_DIM)
        window = queries[:, start : start + 256]
        stacked = jnp.where(own, jnp.concatenate([window] * 4, axis=0), 0.0).astype(BF16)
        scores = lax.dot_general(
            stacked, kv[:, start : start + 256], (((1,), (1,)), ((), ())), preferred_element_type=F32
        )
        counted = mult[...]
        scores = jnp.where(counted > 0.0, scores, masked_score)
        weights = jnp.exp(scores - jnp.max(scores, axis=1, keepdims=True)) * counted
        total = jnp.sum(weights, axis=1, keepdims=True)
        mixed_rows = jnp.dot(
            weights.astype(BF16), kv[:, D_SLIDE + start : D_SLIDE + start + 256], preferred_element_type=F32
        )
        mixed_rows = jnp.where(own, mixed_rows / total, 0.0)
        att[:, start : start + 256] += (
            mixed_rows[0:64] + mixed_rows[64:128] + mixed_rows[128:192] + mixed_rows[192:256]
        )
    result = canvas[mine, :] + jnp.dot(att[...].astype(BF16), wo16[...], preferred_element_type=F32)
    here = iota((SEQ_DEV, D_SLIDE), 0) + s * SEQ_DEV
    out[0] = jnp.where(here < length, result, 0.0)

    for wait in pending:
        wait()


def per_device(
    tiles, mlp_gain, mlp_bias, gate_weight, up_weight, down_weight, layer_scale, final_gain, final_bias,
    patch_weight, patch_bias, slide_gain, slide_bias, w_query, w_key, w_value, w_out, slide_lengths, tile_slot,
):
    hbm = pl.BlockSpec(memory_space=pl.ANY)
    dma = pltpu.SemaphoreType.DMA
    vm = pltpu.VMEM
    return pl.pallas_call(
        kernel,
        out_shape=jax.ShapeDtypeStruct((1, SEQ_DEV, D_SLIDE), F32),
        in_specs=[hbm] * 17 + [pl.BlockSpec(memory_space=pltpu.SMEM)] + [hbm],
        out_specs=pl.BlockSpec(memory_space=pltpu.VMEM),
        scratch_shapes=[
            vm((TILE_DEV, D_TILE), F32), vm((D_TILE,), F32), vm((D_TILE,), F32),
            vm((D_TILE, GROUP), BF16), vm((D_TILE, GROUP), BF16), vm((GROUP, D_TILE), BF16),
            vm((D_TILE,), F32), vm((D_TILE,), F32), vm((D_TILE,), F32),
            vm((D_TILE, D_SLIDE), BF16), vm((D_SLIDE,), F32), vm((D_SLIDE,), F32), vm((D_SLIDE,), F32),
            vm((D_SLIDE, D_SLIDE), F32), vm((D_SLIDE, D_SLIDE), F32),
            vm((D_SLIDE, D_SLIDE), F32), vm((D_SLIDE, D_SLIDE), F32),
            vm((1, TILE_DEV), jnp.int32),
            vm((16, TILE_DEV, D_TILE), BF16), vm((16, TILE_DEV, D_TILE), BF16),
            vm((4, 3, TILE_DEV, D_TILE), BF16), vm((3, TILE_DEV, D_TILE), BF16), vm((3, TILE_DEV, D_TILE), BF16),
            vm((D_SLIDE, 2 * D_SLIDE), BF16), vm((D_SLIDE, D_SLIDE), BF16), vm((D_SLIDE, D_SLIDE), BF16),
            vm((16, 8, 128), F32), vm((16, 8, 128), F32), vm((8, 8, 128), F32),
            vm((16, 16, 384), BF16), vm((16, 16, 384), BF16), vm((8, 128, D_SLIDE), BF16),
            vm((SEQ, 1024), BF16), vm((SEQ, D_SLIDE), F32), vm((SEQ, D_SLIDE), BF16),
            vm((SEQ, 2 * D_SLIDE), BF16), vm((256, SEQ), F32), vm((SEQ_DEV, D_SLIDE), F32),
            dma((18,)), dma((4,)), dma((16,)), dma((16,)), dma((16,)), dma((16,)), dma((4,)), dma((4,)),
            dma((16,)), dma((16,)), dma((8,)), dma((8,)), dma((16,)), dma((16,)), dma((8,)), dma((8,)),
        ],
        compiler_params=pltpu.CompilerParams(
            collective_id=0, has_side_effects=True, vmem_limit_bytes=56 * 2**20
        ),
        name="slide_kernel",
    )(
        tiles, mlp_gain, mlp_bias, gate_weight, up_weight, down_weight, layer_scale,
        final_gain, final_bias, patch_weight, patch_bias, slide_gain, slide_bias,
        w_query, w_key, w_value, w_out, slide_lengths, tile_slot.reshape(1, TILE_DEV),
    )


def solution(mesh):
    both = P(("slide", "tile"))
    placed = (
        P(("slide", "tile"), None), P(), P(), P(None, "tile"), P(None, "tile"), P("tile", None),
        P(), P(), P(), P(), P(), P(), P(), P(), P(), P(), P(), P(), both,
    )
    return jax.shard_map(
        per_device, mesh=mesh, in_specs=placed, out_specs=P("tile", "slide", None), check_vma=False
    )
```

```python
import jax
import jax.numpy as jnp
from jax import lax
from jax.experimental import pallas as pl
from jax.experimental.pallas import tpu as pltpu
from jax.sharding import PartitionSpec as P

D_TILE = 1536
D_SLIDE = 768
HEADS = 16
HEAD_DIM = 48
TILE_DEV = 32
SEQ_DEV = 64
SEQ = 512
GROUP = 256
MESH = pl.DeviceIdType.MESH
F32 = jnp.float32
BF16 = jnp.bfloat16
epsilon = 1e-06
masked_score = -1e30


def layer_norm(values, scale_vec, shift_vec):
    average = jnp.mean(values, axis=-1, keepdims=True)
    centred = values - average
    variance = jnp.mean(centred * centred, axis=-1, keepdims=True)
    return centred * lax.rsqrt(variance + epsilon) * scale_vec + shift_vec


def iota(shape, dim):
    return lax.broadcasted_iota(jnp.int32, shape, dim)


def offset_of(i):
    return i + (i // 2) * (1 - 2 * (i % 2))


def kernel(
    tiles_h, mlp_gain_h, mlp_bias_h, gate_h, up_h, down_h, layer_scale_h, final_gain_h, final_bias_h,
    patch_h, patch_bias_h, slide_gain_h, slide_bias_h, wq_h, wk_h, wv_h, wo_h, lengths, slot_h,
    out,
    tiles, mlp_gain, mlp_bias, gate, up, down, layer_scale, final_gain, final_bias,
    patch, patch_bias, slide_gain, slide_bias, wq, wk, wv, wo, slot,
    rows, part, got1, fold, got2, wkv16, wq16, wo16,
    pos_out, pos_in, pos_all, send_slots, got_slots, slots, one_hot, canvas, normed_all, kv, mult, att,
    load_sem, ag1_s, ag2_s, ag_r, rs1_s, rs1_r, rs2_s, rs2_r,
    pos_s, pos_r, pa_s, pa_r, sl_s, sl_r, dg_s, dg_r,
):
    s = lax.axis_index("slide")
    t = lax.axis_index("tile")
    x, c = s // 2, s % 2
    y, z = t // 4, t % 4

    def first(k):
        return (s, ((y + c * k) % 4) * 4 + (z + (1 - c) * k) % 4)

    def second(k):
        return (s, ((y + (1 - c) * k) % 4) * 4 + (z + c * k) % 4)

    def on_tile(k):
        return (s, ((y + k // 4) % 4) * 4 + (z + k) % 4)

    def on_slide(dx, dc):
        return (((x + dx) % 4) * 2 + (c + dc) % 2, t)

    def remote(src, dst, send_sem, recv_sem, device):
        return pltpu.make_async_remote_copy(
            src_ref=src, dst_ref=dst, send_sem=send_sem, recv_sem=recv_sem,
            device_id=device, device_id_type=MESH,
        )

    pending = []

    def sent(copy, first_k, last_k):
        def one(k, carry):
            copy(k).wait_send()
            return carry

        pending.append(lambda: lax.fori_loop(first_k, last_k, one, 0))

    barrier = pltpu.get_barrier_semaphore()

    def greet(device):
        pl.semaphore_signal(barrier, inc=1, device_id=device, device_id_type=MESH)

    for k in range(1, 4):
        greet(first(k))
        greet(second(k))
    for k in range(1, 8):
        greet(on_slide(k // 2, k % 2))

    pairs = (
        (tiles_h, tiles), (mlp_gain_h, mlp_gain), (mlp_bias_h, mlp_bias),
        (gate_h, gate), (up_h, up), (down_h, down), (slot_h, slot), (layer_scale_h, layer_scale),
        (final_gain_h, final_gain), (final_bias_h, final_bias), (patch_h, patch), (patch_bias_h, patch_bias),
        (wk_h, wk), (wv_h, wv), (wq_h, wq), (wo_h, wo), (slide_gain_h, slide_gain), (slide_bias_h, slide_bias),
    )
    loads = [pltpu.make_async_copy(a, b, load_sem.at[i]) for i, (a, b) in enumerate(pairs)]
    for load in loads:
        load.start()
    for i in range(3):
        loads[i].wait()
    rows[0] = layer_norm(tiles[...], mlp_gain[...], mlp_bias[...]).astype(BF16)

    pl.semaphore_wait(barrier, 13)

    def ag1(j):
        return remote(rows.at[0], rows.at[4 * j], ag1_s.at[j], ag_r.at[4 * j], first(offset_of(j)))

    for j in range(1, 4):
        ag1(j).start()
        pending.append(ag1(j).wait_send)

    def ag2(i, j):
        return remote(
            rows.at[4 * j], rows.at[4 * j + i], ag2_s.at[4 * j + i], ag_r.at[4 * j + i], second(offset_of(i))
        )

    def side_of(j):
        return ((j + 1) // 2) % 2

    def pass_on(j):
        m = side_of(j)
        return remote(
            rows.at[4 * j + 1 + m], rows.at[4 * j + 3], ag2_s.at[4 * j + 3], ag_r.at[4 * j + 3], second(1 + 2 * m)
        )

    def spread(j):
        for i in range(1, 3):
            ag2(i, j).start()
            pending.append(ag2(i, j).wait_send)

    def relay(j):
        ag2(1 + side_of(j), j).wait_recv()
        pass_on(j).start()

    def far_last():
        return remote(rows.at[12], rows.at[15], ag2_s.at[15], ag_r.at[15], second(2))

    spread(0)
    for j in range(1, 3):
        ag1(j).wait_recv()
        spread(j)
    relay(0)
    ag1(3).wait_recv()
    far_last().start()
    spread(3)
    pending.append(far_last().wait_send)
    relay(1)
    relay(2)
    for j in range(3):
        pending.append(pass_on(j).wait_send)
    for i in range(3, 6):
        loads[i].wait()

    def rs1(i, j):
        return remote(
            part.at[4 * j + i], got1.at[j, i - 1], rs1_s.at[4 * j + i], rs1_r.at[4 * j + i], second(4 - offset_of(i))
        )

    def batch(j, carry):
        ag2(2 - side_of(j), j).wait_recv()
        pass_on(j).wait_recv()

        @pl.when(j == 3)
        def _():
            ag2(1, 3).wait_recv()

        block = rows[pl.ds(4 * j, 4)].reshape(128, D_TILE)
        gate_out = jnp.dot(block, gate[...], preferred_element_type=F32)
        up_out = jnp.dot(block, up[...], preferred_element_type=F32)
        hidden = (gate_out / (1.0 + jnp.exp(-gate_out)) * up_out).astype(BF16)
        part[pl.ds(4 * j, 4)] = (
            jnp.dot(hidden, down[...], preferred_element_type=F32).astype(BF16).reshape(4, TILE_DEV, D_TILE)
        )
        for i in (3, 1, 2):
            rs1(i, j).start()
        return carry

    lax.fori_loop(0, 4, batch, 0)
    for j in range(4):
        for i in range(1, 4):
            pending.append(rs1(i, j).wait_send)

    loads[6].wait()
    spot = slot[...]
    row_id = iota((128, TILE_DEV), 0)
    match = (spot // 512 == row_id // 8) & ((spot // 64) % 8 == row_id % 8)
    place = jnp.sum(jnp.where(match, (spot % 512 + 1).astype(F32), 0.0), axis=1, keepdims=True)
    pos_out[...] = jnp.broadcast_to(place, (128, 128)).reshape(16, 8, 128)
    pos_in[0] = pos_out[t]

    def pos_copy(k):
        return remote(pos_out.at[on_tile(k)[1]], pos_in.at[k], pos_s.at[k], pos_r.at[k], on_tile(k))

    def pos_start(k, carry):
        pos_copy(k).start()
        return carry

    lax.fori_loop(1, 16, pos_start, 0)
    sent(pos_copy, 1, 16)

    for i in range(12, 16):
        loads[i].wait()

    def convert(k, carry):
        at = pl.ds(pl.multiple_of(k * 128, 128), 128)
        wkv16[at, 0:D_SLIDE] = wk[at, :].astype(BF16)
        wkv16[at, D_SLIDE : 2 * D_SLIDE] = wv[at, :].astype(BF16)
        wq16[at, :] = wq[at, :].astype(BF16)
        wo16[at, :] = wo[at, :].astype(BF16)
        return carry

    lax.fori_loop(0, 6, convert, 0)

    length = lengths[t]
    row = iota((256, SEQ), 0)
    key = iota((256, SEQ), 1)
    head, query = row // 64, row % 64
    weight = (
        1.0
        + jnp.where((query % 2 == head % 2) & (key % 2 == head % 2), 1.0, 0.0)
        + jnp.where((query % 4 == head) & (key % 4 == head), 1.0, 0.0)
    )
    mult[...] = jnp.where(key < length, weight, 0.0)

    def rs2(j):
        return remote(fold.at[j - 1], got2.at[j - 1], rs2_s.at[j], rs2_r.at[j], first(4 - offset_of(j)))

    def line_sum(j):
        for i in range(1, 4):
            rs1(i, j).wait_recv()
        return (
            part[4 * j].astype(F32) + got1[j, 0].astype(F32) + got1[j, 1].astype(F32) + got1[j, 2].astype(F32)
        )

    for j in range(1, 4):
        fold[j - 1] = line_sum(j).astype(BF16)
        rs2(j).start()
        pending.append(rs2(j).wait_send)
    mixed = line_sum(0)

    def pos_wait(k, carry):
        pos_copy(k).wait_recv()
        return carry

    lax.fori_loop(1, 16, pos_wait, 0)
    turned = jnp.transpose(pos_in[...].reshape(128, 128))
    pos_all[0] = turned[0:8]

    def pa_copy(k):
        return remote(pos_all.at[0], pos_all.at[k], pa_s.at[k], pa_r.at[k], on_slide(k // 2, k % 2))

    def pa_start(k, carry):
        pa_copy(k).start()
        return carry

    lax.fori_loop(1, 8, pa_start, 0)
    sent(pa_copy, 1, 8)

    for i in range(7, 12):
        loads[i].wait()
    for j in range(1, 4):
        rs2(j).wait_recv()
    mixed = mixed + got2[0].astype(F32) + got2[1].astype(F32) + got2[2].astype(F32)
    final = layer_norm(tiles[...] + layer_scale[...] * mixed, final_gain[...], final_bias[...]).astype(BF16)
    embed = (jnp.dot(final, patch[...], preferred_element_type=F32) + patch_bias[...]).astype(BF16)

    slot_id = iota((256, TILE_DEV), 0)
    hit = (spot // 512 == slot_id // 16) & ((spot // 64) % 8 == slot_id % 8)
    left = jnp.where(hit & (slot_id % 16 < 8), 1.0, 0.0).astype(BF16)
    right = jnp.where(hit & (slot_id % 16 >= 8), 1.0, 0.0).astype(BF16)
    send_slots[...] = (
        (
            jnp.dot(left, embed[:, 0:384], preferred_element_type=F32)
            + jnp.dot(right, embed[:, 384:768], preferred_element_type=F32)
        )
        .astype(BF16)
        .reshape(16, 16, 384)
    )

    def slot_copy(k):
        return remote(send_slots.at[on_tile(k)[1]], got_slots.at[k], sl_s.at[k], sl_r.at[k], on_tile(k))

    def slot_start(k, carry):
        slot_copy(k).start()
        return carry

    lax.fori_loop(1, 16, slot_start, 0)
    sent(slot_copy, 1, 16)
    got_slots[0] = send_slots[t]

    def pa_wait(k, carry):
        pa_copy(k).wait_recv()
        return carry

    lax.fori_loop(1, 8, pa_wait, 0)
    position = (iota((SEQ, 128), 0) + 1).astype(F32)
    for k in range(8):
        one_hot[:, k * 128 : (k + 1) * 128] = jnp.where(position == pos_all[k][0:1], 1.0, 0.0).astype(BF16)

    def along(e, q, dx):
        return remote(slots.at[0, q], slots.at[e, q], dg_s.at[4 * e + q], dg_r.at[4 * e + q], on_slide(dx, 0))

    def far_on(q):
        return remote(
            slots.at[2 + 4 * c, q], slots.at[4, q], dg_s.at[16 + q], dg_r.at[16 + q], on_slide(1 + 2 * c, 0)
        )

    def near(e, q):
        at = 4 * e + 4 + q
        return remote(slots.at[e, q], slots.at[e + 1, q], dg_s.at[at], dg_r.at[at], on_slide(0, 1))

    order = (0, 1, 3, 2)
    for q in order:
        for k in range(4 * q, 4 * q + 4):
            if k > 0:
                slot_copy(k).wait_recv()
        wide = got_slots[4 * q : 4 * q + 4].astype(F32)
        slots[0, q, :, 0:384] = wide[:, 0:8, :].reshape(32, 384).astype(BF16)
        slots[0, q, :, 384:768] = wide[:, 8:16, :].reshape(32, 384).astype(BF16)
        if q == order[3]:
            along(4, q, 2).start()
            pending.append(along(4, q, 2).wait_send)
        along(2, q, 1).start()
        along(6, q, 3).start()
        near(0, q).start()
        pending.append(along(2, q, 1).wait_send)
        pending.append(along(6, q, 3).wait_send)
        pending.append(near(0, q).wait_send)

    def came(e, q):
        along(e, q, 0).wait_recv()
        near(e, q).start()
        pending.append(near(e, q).wait_send)

    for q in order:
        along(2 + 4 * c, q, 0).wait_recv()
        if q != order[3]:
            far_on(q).start()
            pending.append(far_on(q).wait_send)
        near(2 + 4 * c, q).start()
        pending.append(near(2 + 4 * c, q).wait_send)
        came(6 - 4 * c, q)

    def place_pair(k):
        return jnp.dot(
            one_hot[:, k * 128 : (k + 2) * 128], slots[k : k + 2].reshape(256, D_SLIDE), preferred_element_type=F32
        )

    for q in order:
        near(0, q).wait_recv()
    canvas[...] = place_pair(0)
    for q in order:
        came(4, q)
    for k in (2, 6, 4):
        for q in order:
            near(k, q).wait_recv()
        canvas[...] += place_pair(k)
    for i in range(16, 18):
        loads[i].wait()
    normed_all[...] = layer_norm(canvas[...], slide_gain[...], slide_bias[...]).astype(BF16)
    mine = pl.ds(pl.multiple_of(s * SEQ_DEV, SEQ_DEV), SEQ_DEV)
    kv[...] = jnp.dot(normed_all[...], wkv16[...], preferred_element_type=F32).astype(BF16)
    queries = jnp.dot(normed_all[mine, :], wq16[...], preferred_element_type=F32) * HEAD_DIM ** (-0.5)

    head_row = iota((256, 256), 0) // 64
    lane = iota((256, 256), 1)
    att[...] = jnp.zeros_like(att)
    for w, start in enumerate((0, 128, 384, 512)):
        low = (4 * w + head_row) * HEAD_DIM - start
        own = (lane >= low) & (lane < low + HEAD_DIM)
        window = queries[:, start : start + 256]
        stacked = jnp.where(own, jnp.concatenate([window] * 4, axis=0), 0.0).astype(BF16)
        scores = lax.dot_general(
            stacked, kv[:, start : start + 256], (((1,), (1,)), ((), ())), preferred_element_type=F32
        )
        counted = mult[...]
        scores = jnp.where(counted > 0.0, scores, masked_score)
        weights = jnp.exp(scores - jnp.max(scores, axis=1, keepdims=True)) * counted
        total = jnp.sum(weights, axis=1, keepdims=True)
        mixed_rows = jnp.dot(
            weights.astype(BF16), kv[:, D_SLIDE + start : D_SLIDE + start + 256], preferred_element_type=F32
        )
        mixed_rows = jnp.where(own, mixed_rows / total, 0.0)
        att[:, start : start + 256] += (
            mixed_rows[0:64] + mixed_rows[64:128] + mixed_rows[128:192] + mixed_rows[192:256]
        )
    result = canvas[mine, :] + jnp.dot(att[...].astype(BF16), wo16[...], preferred_element_type=F32)
    here = iota((SEQ_DEV, D_SLIDE), 0) + s * SEQ_DEV
    out[0] = jnp.where(here < length, result, 0.0)

    for wait in pending:
        wait()


def per_device(
    tiles, mlp_gain, mlp_bias, gate_weight, up_weight, down_weight, layer_scale, final_gain, final_bias,
    patch_weight, patch_bias, slide_gain, slide_bias, w_query, w_key, w_value, w_out, slide_lengths, tile_slot,
):
    hbm = pl.BlockSpec(memory_space=pl.ANY)
    dma = pltpu.SemaphoreType.DMA
    vm = pltpu.VMEM
    return pl.pallas_call(
        kernel,
        out_shape=jax.ShapeDtypeStruct((1, SEQ_DEV, D_SLIDE), F32),
        in_specs=[hbm] * 17 + [pl.BlockSpec(memory_space=pltpu.SMEM)] + [hbm],
        out_specs=pl.BlockSpec(memory_space=pltpu.VMEM),
        scratch_shapes=[
            vm((TILE_DEV, D_TILE), F32), vm((D_TILE,), F32), vm((D_TILE,), F32),
            vm((D_TILE, GROUP), BF16), vm((D_TILE, GROUP), BF16), vm((GROUP, D_TILE), BF16),
            vm((D_TILE,), F32), vm((D_TILE,), F32), vm((D_TILE,), F32),
            vm((D_TILE, D_SLIDE), BF16), vm((D_SLIDE,), F32), vm((D_SLIDE,), F32), vm((D_SLIDE,), F32),
            vm((D_SLIDE, D_SLIDE), F32), vm((D_SLIDE, D_SLIDE), F32),
            vm((D_SLIDE, D_SLIDE), F32), vm((D_SLIDE, D_SLIDE), F32),
            vm((1, TILE_DEV), jnp.int32),
            vm((16, TILE_DEV, D_TILE), BF16), vm((16, TILE_DEV, D_TILE), BF16),
            vm((4, 3, TILE_DEV, D_TILE), BF16), vm((3, TILE_DEV, D_TILE), BF16), vm((3, TILE_DEV, D_TILE), BF16),
            vm((D_SLIDE, 2 * D_SLIDE), BF16), vm((D_SLIDE, D_SLIDE), BF16), vm((D_SLIDE, D_SLIDE), BF16),
            vm((16, 8, 128), F32), vm((16, 8, 128), F32), vm((8, 8, 128), F32),
            vm((16, 16, 384), BF16), vm((16, 16, 384), BF16), vm((8, 4, 32, D_SLIDE), BF16),
            vm((SEQ, 1024), BF16), vm((SEQ, D_SLIDE), F32), vm((SEQ, D_SLIDE), BF16),
            vm((SEQ, 2 * D_SLIDE), BF16), vm((256, SEQ), F32), vm((SEQ_DEV, D_SLIDE), F32),
            dma((18,)), dma((4,)), dma((16,)), dma((16,)), dma((16,)), dma((16,)), dma((4,)), dma((4,)),
            dma((16,)), dma((16,)), dma((8,)), dma((8,)), dma((16,)), dma((16,)), dma((32,)), dma((32,)),
        ],
        compiler_params=pltpu.CompilerParams(
            collective_id=0, has_side_effects=True, vmem_limit_bytes=56 * 2**20
        ),
        name="slide_kernel",
    )(
        tiles, mlp_gain, mlp_bias, gate_weight, up_weight, down_weight, layer_scale,
        final_gain, final_bias, patch_weight, patch_bias, slide_gain, slide_bias,
        w_query, w_key, w_value, w_out, slide_lengths, tile_slot.reshape(1, TILE_DEV),
    )


def solution(mesh):
    both = P(("slide", "tile"))
    placed = (
        P(("slide", "tile"), None), P(), P(), P(None, "tile"), P(None, "tile"), P("tile", None),
        P(), P(), P(), P(), P(), P(), P(), P(), P(), P(), P(), P(), both,
    )
    return jax.shard_map(
        per_device, mesh=mesh, in_specs=placed, out_specs=P("tile", "slide", None), check_vma=False
    )
```

```python
import jax
import jax.numpy as jnp
from jax import lax
from jax.experimental import pallas as pl
from jax.experimental.pallas import tpu as pltpu
from jax.sharding import PartitionSpec as P

D_TILE = 1536
D_SLIDE = 768
HEADS = 16
HEAD_DIM = 48
TILE_DEV = 32
SEQ_DEV = 64
SEQ = 512
GROUP = 256
MESH = pl.DeviceIdType.MESH
F32 = jnp.float32
BF16 = jnp.bfloat16
epsilon = 1e-06
masked_score = -1e30


def layer_norm(values, scale_vec, shift_vec):
    average = jnp.mean(values, axis=-1, keepdims=True)
    centred = values - average
    variance = jnp.mean(centred * centred, axis=-1, keepdims=True)
    return centred * lax.rsqrt(variance + epsilon) * scale_vec + shift_vec


def iota(shape, dim):
    return lax.broadcasted_iota(jnp.int32, shape, dim)


def offset_of(i):
    return i + (i // 2) * (1 - 2 * (i % 2))


def kernel(
    tiles_h, mlp_gain_h, mlp_bias_h, gate_h, up_h, down_h, layer_scale_h, final_gain_h, final_bias_h,
    patch_h, patch_bias_h, slide_gain_h, slide_bias_h, wq_h, wk_h, wv_h, wo_h, lengths, slot_h,
    out,
    tiles, mlp_gain, mlp_bias, gate, up, down, layer_scale, final_gain, final_bias,
    patch, patch_bias, slide_gain, slide_bias, wq, wk, wv, wo, slot,
    rows, part, got1, fold, got2, wkv16, wq16, wo16,
    pos_out, pos_in, pos_all, send_slots, got_slots, slots, one_hot, canvas, normed_all, kv, mult, att,
    load_sem, ag1_s, ag2_s, ag_r, rs1_s, rs1_r, rs2_s, rs2_r,
    pos_s, pos_r, pa_s, pa_r, sl_s, sl_r, dg_s, dg_r,
):
    s = lax.axis_index("slide")
    t = lax.axis_index("tile")
    x, c = s // 2, s % 2
    y, z = t // 4, t % 4

    def first(k):
        return (s, ((y + c * k) % 4) * 4 + (z + (1 - c) * k) % 4)

    def second(k):
        return (s, ((y + (1 - c) * k) % 4) * 4 + (z + c * k) % 4)

    def on_tile(k):
        return (s, ((y + k // 4) % 4) * 4 + (z + k) % 4)

    def on_slide(dx, dc):
        return (((x + dx) % 4) * 2 + (c + dc) % 2, t)

    def remote(src, dst, send_sem, recv_sem, device):
        return pltpu.make_async_remote_copy(
            src_ref=src, dst_ref=dst, send_sem=send_sem, recv_sem=recv_sem,
            device_id=device, device_id_type=MESH,
        )

    pending = []

    def sent(copy, first_k, last_k):
        def one(k, carry):
            copy(k).wait_send()
            return carry

        pending.append(lambda: lax.fori_loop(first_k, last_k, one, 0))

    barrier = pltpu.get_barrier_semaphore()

    def greet(device):
        pl.semaphore_signal(barrier, inc=1, device_id=device, device_id_type=MESH)

    for k in range(1, 4):
        greet(first(k))
        greet(second(k))
    for k in range(1, 8):
        greet(on_slide(k // 2, k % 2))

    pairs = (
        (tiles_h, tiles), (mlp_gain_h, mlp_gain), (mlp_bias_h, mlp_bias),
        (gate_h, gate), (up_h, up), (down_h, down), (slot_h, slot), (layer_scale_h, layer_scale),
        (final_gain_h, final_gain), (final_bias_h, final_bias), (patch_h, patch), (patch_bias_h, patch_bias),
        (wk_h, wk), (wv_h, wv), (wq_h, wq), (wo_h, wo), (slide_gain_h, slide_gain), (slide_bias_h, slide_bias),
    )
    loads = [pltpu.make_async_copy(a, b, load_sem.at[i]) for i, (a, b) in enumerate(pairs)]
    for load in loads:
        load.start()
    for i in range(3):
        loads[i].wait()
    rows[0] = layer_norm(tiles[...], mlp_gain[...], mlp_bias[...]).astype(BF16)

    pl.semaphore_wait(barrier, 13)

    def ag1(j):
        return remote(rows.at[0], rows.at[4 * j], ag1_s.at[j], ag_r.at[4 * j], first(offset_of(j)))

    for j in range(1, 4):
        ag1(j).start()
        pending.append(ag1(j).wait_send)

    def ag2(i, j):
        return remote(
            rows.at[4 * j], rows.at[4 * j + i], ag2_s.at[4 * j + i], ag_r.at[4 * j + i], second(offset_of(i))
        )

    def spread(j):
        for i in range(1, 3):
            ag2(i, j).start()
            pending.append(ag2(i, j).wait_send)

    def far_chunk(j):
        return remote(rows.at[4 * j], rows.at[4 * j + 3], ag2_s.at[4 * j + 3], ag_r.at[4 * j + 3], second(2))

    spread(0)
    far_chunk(0).start()
    ag1(1).wait_recv()
    spread(1)
    far_chunk(1).start()
    ag1(2).wait_recv()
    spread(2)
    far_chunk(2).start()
    ag1(3).wait_recv()
    far_chunk(3).start()
    spread(3)
    pending.append(far_chunk(0).wait_send)
    pending.append(far_chunk(1).wait_send)
    pending.append(far_chunk(2).wait_send)
    pending.append(far_chunk(3).wait_send)
    for i in range(3, 6):
        loads[i].wait()

    def rs1(i, j):
        return remote(
            part.at[4 * j + i], got1.at[j, i - 1], rs1_s.at[4 * j + i], rs1_r.at[4 * j + i], second(4 - offset_of(i))
        )

    def batch(j, carry):
        ag2(1, j).wait_recv()
        ag2(2, j).wait_recv()
        far_chunk(j).wait_recv()

        block = rows[pl.ds(4 * j, 4)].reshape(128, D_TILE)
        gate_out = jnp.dot(block, gate[...], preferred_element_type=F32)
        up_out = jnp.dot(block, up[...], preferred_element_type=F32)
        hidden = (gate_out / (1.0 + jnp.exp(-gate_out)) * up_out).astype(BF16)
        part[pl.ds(4 * j, 4)] = (
            jnp.dot(hidden, down[...], preferred_element_type=F32).astype(BF16).reshape(4, TILE_DEV, D_TILE)
        )
        for i in (3, 1, 2):
            rs1(i, j).start()
        return carry

    lax.fori_loop(0, 4, batch, 0)
    for j in range(4):
        for i in range(1, 4):
            pending.append(rs1(i, j).wait_send)

    loads[6].wait()
    spot = slot[...]
    row_id = iota((128, TILE_DEV), 0)
    match = (spot // 512 == row_id // 8) & ((spot // 64) % 8 == row_id % 8)
    place = jnp.sum(jnp.where(match, (spot % 512 + 1).astype(F32), 0.0), axis=1, keepdims=True)
    pos_out[...] = jnp.broadcast_to(place, (128, 128)).reshape(16, 8, 128)
    pos_in[0] = pos_out[t]

    def pos_copy(k):
        return remote(pos_out.at[on_tile(k)[1]], pos_in.at[k], pos_s.at[k], pos_r.at[k], on_tile(k))

    def pos_start(k, carry):
        pos_copy(k).start()
        return carry

    lax.fori_loop(1, 16, pos_start, 0)
    sent(pos_copy, 1, 16)

    for i in range(12, 16):
        loads[i].wait()

    def convert(k, carry):
        at = pl.ds(pl.multiple_of(k * 128, 128), 128)
        wkv16[at, 0:D_SLIDE] = wk[at, :].astype(BF16)
        wkv16[at, D_SLIDE : 2 * D_SLIDE] = wv[at, :].astype(BF16)
        wq16[at, :] = wq[at, :].astype(BF16)
        wo16[at, :] = wo[at, :].astype(BF16)
        return carry

    lax.fori_loop(0, 6, convert, 0)

    length = lengths[t]
    row = iota((256, SEQ), 0)
    key = iota((256, SEQ), 1)
    head, query = row // 64, row % 64
    weight = (
        1.0
        + jnp.where((query % 2 == head % 2) & (key % 2 == head % 2), 1.0, 0.0)
        + jnp.where((query % 4 == head) & (key % 4 == head), 1.0, 0.0)
    )
    mult[...] = jnp.where(key < length, weight, 0.0)

    def rs2(j):
        return remote(fold.at[j - 1], got2.at[j - 1], rs2_s.at[j], rs2_r.at[j], first(4 - offset_of(j)))

    def line_sum(j):
        for i in range(1, 4):
            rs1(i, j).wait_recv()
        return (
            part[4 * j].astype(F32) + got1[j, 0].astype(F32) + got1[j, 1].astype(F32) + got1[j, 2].astype(F32)
        )

    for j in range(1, 4):
        fold[j - 1] = line_sum(j).astype(BF16)
        rs2(j).start()
        pending.append(rs2(j).wait_send)
    mixed = line_sum(0)

    def pos_wait(k, carry):
        pos_copy(k).wait_recv()
        return carry

    lax.fori_loop(1, 16, pos_wait, 0)
    turned = jnp.transpose(pos_in[...].reshape(128, 128))
    pos_all[0] = turned[0:8]

    def pa_copy(k):
        return remote(pos_all.at[0], pos_all.at[k], pa_s.at[k], pa_r.at[k], on_slide(k // 2, k % 2))

    def pa_start(k, carry):
        pa_copy(k).start()
        return carry

    lax.fori_loop(1, 8, pa_start, 0)
    sent(pa_copy, 1, 8)

    for i in range(7, 12):
        loads[i].wait()
    for j in range(1, 4):
        rs2(j).wait_recv()
    mixed = mixed + got2[0].astype(F32) + got2[1].astype(F32) + got2[2].astype(F32)
    final = layer_norm(tiles[...] + layer_scale[...] * mixed, final_gain[...], final_bias[...]).astype(BF16)
    embed = (jnp.dot(final, patch[...], preferred_element_type=F32) + patch_bias[...]).astype(BF16)

    slot_id = iota((256, TILE_DEV), 0)
    hit = (spot // 512 == slot_id // 16) & ((spot // 64) % 8 == slot_id % 8)
    left = jnp.where(hit & (slot_id % 16 < 8), 1.0, 0.0).astype(BF16)
    right = jnp.where(hit & (slot_id % 16 >= 8), 1.0, 0.0).astype(BF16)
    send_slots[...] = (
        (
            jnp.dot(left, embed[:, 0:384], preferred_element_type=F32)
            + jnp.dot(right, embed[:, 384:768], preferred_element_type=F32)
        )
        .astype(BF16)
        .reshape(16, 16, 384)
    )

    def slot_copy(k):
        return remote(send_slots.at[on_tile(k)[1]], got_slots.at[k], sl_s.at[k], sl_r.at[k], on_tile(k))

    def slot_start(k, carry):
        slot_copy(k).start()
        return carry

    lax.fori_loop(1, 16, slot_start, 0)
    sent(slot_copy, 1, 16)
    got_slots[0] = send_slots[t]

    def pa_wait(k, carry):
        pa_copy(k).wait_recv()
        return carry

    lax.fori_loop(1, 8, pa_wait, 0)
    position = (iota((SEQ, 128), 0) + 1).astype(F32)
    for k in range(8):
        one_hot[:, k * 128 : (k + 1) * 128] = jnp.where(position == pos_all[k][0:1], 1.0, 0.0).astype(BF16)

    def along(e, q, dx):
        return remote(slots.at[0, q], slots.at[e, q], dg_s.at[4 * e + q], dg_r.at[4 * e + q], on_slide(dx, 0))

    def near(e, q):
        at = 4 * e + 4 + q
        return remote(slots.at[e, q], slots.at[e + 1, q], dg_s.at[at], dg_r.at[at], on_slide(0, 1))

    order = (0, 1, 3, 2)
    for q in order:
        for k in range(4 * q, 4 * q + 4):
            if k > 0:
                slot_copy(k).wait_recv()
        wide = got_slots[4 * q : 4 * q + 4].astype(F32)
        slots[0, q, :, 0:384] = wide[:, 0:8, :].reshape(32, 384).astype(BF16)
        slots[0, q, :, 384:768] = wide[:, 8:16, :].reshape(32, 384).astype(BF16)
        along(4, q, 2).start()
        pending.append(along(4, q, 2).wait_send)
        along(2, q, 1).start()
        along(6, q, 3).start()
        near(0, q).start()
        pending.append(along(2, q, 1).wait_send)
        pending.append(along(6, q, 3).wait_send)
        pending.append(near(0, q).wait_send)

    def came(e, q):
        along(e, q, 0).wait_recv()
        near(e, q).start()
        pending.append(near(e, q).wait_send)

    for q in order:
        along(2 + 4 * c, q, 0).wait_recv()
        near(2 + 4 * c, q).start()
        pending.append(near(2 + 4 * c, q).wait_send)
        came(6 - 4 * c, q)

    def place_pair(k):
        return jnp.dot(
            one_hot[:, k * 128 : (k + 2) * 128], slots[k : k + 2].reshape(256, D_SLIDE), preferred_element_type=F32
        )

    for q in order:
        near(0, q).wait_recv()
    canvas[...] = place_pair(0)
    for q in order:
        came(4, q)
    for k in (2, 6, 4):
        for q in order:
            near(k, q).wait_recv()
        canvas[...] += place_pair(k)
    for i in range(16, 18):
        loads[i].wait()
    normed_all[...] = layer_norm(canvas[...], slide_gain[...], slide_bias[...]).astype(BF16)
    mine = pl.ds(pl.multiple_of(s * SEQ_DEV, SEQ_DEV), SEQ_DEV)
    kv[...] = jnp.dot(normed_all[...], wkv16[...], preferred_element_type=F32).astype(BF16)
    queries = jnp.dot(normed_all[mine, :], wq16[...], preferred_element_type=F32) * HEAD_DIM ** (-0.5)

    head_row = iota((256, 256), 0) // 64
    lane = iota((256, 256), 1)
    att[...] = jnp.zeros_like(att)
    for w, start in enumerate((0, 128, 384, 512)):
        low = (4 * w + head_row) * HEAD_DIM - start
        own = (lane >= low) & (lane < low + HEAD_DIM)
        window = queries[:, start : start + 256]
        stacked = jnp.where(own, jnp.concatenate([window] * 4, axis=0), 0.0).astype(BF16)
        scores = lax.dot_general(
            stacked, kv[:, start : start + 256], (((1,), (1,)), ((), ())), preferred_element_type=F32
        )
        counted = mult[...]
        scores = jnp.where(counted > 0.0, scores, masked_score)
        weights = jnp.exp(scores - jnp.max(scores, axis=1, keepdims=True)) * counted
        total = jnp.sum(weights, axis=1, keepdims=True)
        mixed_rows = jnp.dot(
            weights.astype(BF16), kv[:, D_SLIDE + start : D_SLIDE + start + 256], preferred_element_type=F32
        )
        mixed_rows = jnp.where(own, mixed_rows / total, 0.0)
        att[:, start : start + 256] += (
            mixed_rows[0:64] + mixed_rows[64:128] + mixed_rows[128:192] + mixed_rows[192:256]
        )
    result = canvas[mine, :] + jnp.dot(att[...].astype(BF16), wo16[...], preferred_element_type=F32)
    here = iota((SEQ_DEV, D_SLIDE), 0) + s * SEQ_DEV
    out[0] = jnp.where(here < length, result, 0.0)

    for wait in pending:
        wait()


def per_device(
    tiles, mlp_gain, mlp_bias, gate_weight, up_weight, down_weight, layer_scale, final_gain, final_bias,
    patch_weight, patch_bias, slide_gain, slide_bias, w_query, w_key, w_value, w_out, slide_lengths, tile_slot,
):
    hbm = pl.BlockSpec(memory_space=pl.ANY)
    dma = pltpu.SemaphoreType.DMA
    vm = pltpu.VMEM
    return pl.pallas_call(
        kernel,
        out_shape=pltpu.VMEM((1, SEQ_DEV, D_SLIDE), F32),
        in_specs=[hbm] * 17 + [pl.BlockSpec(memory_space=pltpu.SMEM)] + [hbm],
        out_specs=pl.BlockSpec(memory_space=pltpu.VMEM),
        scratch_shapes=[
            vm((TILE_DEV, D_TILE), F32), vm((D_TILE,), F32), vm((D_TILE,), F32),
            vm((D_TILE, GROUP), BF16), vm((D_TILE, GROUP), BF16), vm((GROUP, D_TILE), BF16),
            vm((D_TILE,), F32), vm((D_TILE,), F32), vm((D_TILE,), F32),
            vm((D_TILE, D_SLIDE), BF16), vm((D_SLIDE,), F32), vm((D_SLIDE,), F32), vm((D_SLIDE,), F32),
            vm((D_SLIDE, D_SLIDE), F32), vm((D_SLIDE, D_SLIDE), F32),
            vm((D_SLIDE, D_SLIDE), F32), vm((D_SLIDE, D_SLIDE), F32),
            vm((1, TILE_DEV), jnp.int32),
            vm((16, TILE_DEV, D_TILE), BF16), vm((16, TILE_DEV, D_TILE), BF16),
            vm((4, 3, TILE_DEV, D_TILE), BF16), vm((3, TILE_DEV, D_TILE), BF16), vm((3, TILE_DEV, D_TILE), BF16),
            vm((D_SLIDE, 2 * D_SLIDE), BF16), vm((D_SLIDE, D_SLIDE), BF16), vm((D_SLIDE, D_SLIDE), BF16),
            vm((16, 8, 128), F32), vm((16, 8, 128), F32), vm((8, 8, 128), F32),
            vm((16, 16, 384), BF16), vm((16, 16, 384), BF16), vm((8, 4, 32, D_SLIDE), BF16),
            vm((SEQ, 1024), BF16), vm((SEQ, D_SLIDE), F32), vm((SEQ, D_SLIDE), BF16),
            vm((SEQ, 2 * D_SLIDE), BF16), vm((256, SEQ), F32), vm((SEQ_DEV, D_SLIDE), F32),
            dma((18,)), dma((4,)), dma((16,)), dma((16,)), dma((16,)), dma((16,)), dma((4,)), dma((4,)),
            dma((16,)), dma((16,)), dma((8,)), dma((8,)), dma((16,)), dma((16,)), dma((32,)), dma((32,)),
        ],
        compiler_params=pltpu.CompilerParams(
            collective_id=0, has_side_effects=True, vmem_limit_bytes=56 * 2**20
        ),
        name="slide_kernel",
    )(
        tiles, mlp_gain, mlp_bias, gate_weight, up_weight, down_weight, layer_scale,
        final_gain, final_bias, patch_weight, patch_bias, slide_gain, slide_bias,
        w_query, w_key, w_value, w_out, slide_lengths, tile_slot.reshape(1, TILE_DEV),
    )


def solution(mesh):
    both = P(("slide", "tile"))
    placed = (
        P(("slide", "tile"), None), P(), P(), P(None, "tile"), P(None, "tile"), P("tile", None),
        P(), P(), P(), P(), P(), P(), P(), P(), P(), P(), P(), P(), both,
    )
    return jax.shard_map(
        per_device, mesh=mesh, in_specs=placed, out_specs=P("tile", "slide", None), check_vma=False
    )
```

```python
import jax
import jax.numpy as jnp
from jax import lax
from jax.experimental import pallas as pl
from jax.experimental.pallas import tpu as pltpu
from jax.sharding import PartitionSpec as P

D_TILE = 1536
D_SLIDE = 768
HEADS = 16
HEAD_DIM = 48
TILE_DEV = 32
SEQ_DEV = 64
SEQ = 512
GROUP = 256
MESH = pl.DeviceIdType.MESH
F32 = jnp.float32
BF16 = jnp.bfloat16
epsilon = 1e-06
masked_score = -1e30


def layer_norm(values, scale_vec, shift_vec):
    average = jnp.mean(values, axis=-1, keepdims=True)
    centred = values - average
    variance = jnp.mean(centred * centred, axis=-1, keepdims=True)
    return centred * lax.rsqrt(variance + epsilon) * scale_vec + shift_vec


def iota(shape, dim):
    return lax.broadcasted_iota(jnp.int32, shape, dim)


def offset_of(i):
    return i + (i // 2) * (1 - 2 * (i % 2))


def kernel(
    tiles_h, mlp_gain_h, mlp_bias_h, gate_h, up_h, down_h, layer_scale_h, final_gain_h, final_bias_h,
    patch_h, patch_bias_h, slide_gain_h, slide_bias_h, wq_h, wk_h, wv_h, wo_h, lengths_h, slot_h,
    out,
    tiles, mlp_gain, mlp_bias, gate, up, down, layer_scale, final_gain, final_bias,
    patch, patch_bias, slide_gain, slide_bias, wq, wk, wv, wo, slot, lengths,
    rows, part, got1, fold, got2, wkv16, wq16, wo16,
    pos_out, pos_in, pos_all, send_slots, got_slots, slots, one_hot, canvas, normed_all, kv, mult, att,
    load_sem, ag1_s, ag2_s, ag_r, rs1_s, rs1_r, rs2_s, rs2_r,
    pos_s, pos_r, pa_s, pa_r, sl_s, sl_r, dg_s, dg_r,
):
    s = lax.axis_index("slide")
    t = lax.axis_index("tile")
    x, c = s // 2, s % 2
    y, z = t // 4, t % 4

    def first(k):
        return (s, ((y + c * k) % 4) * 4 + (z + (1 - c) * k) % 4)

    def second(k):
        return (s, ((y + (1 - c) * k) % 4) * 4 + (z + c * k) % 4)

    def on_tile(k):
        return (s, ((y + k // 4) % 4) * 4 + (z + k) % 4)

    def on_slide(dx, dc):
        return (((x + dx) % 4) * 2 + (c + dc) % 2, t)

    def remote(src, dst, send_sem, recv_sem, device):
        return pltpu.make_async_remote_copy(
            src_ref=src, dst_ref=dst, send_sem=send_sem, recv_sem=recv_sem,
            device_id=device, device_id_type=MESH,
        )

    pending = []

    def drain():
        for wait in pending:
            wait()
        pending.clear()

    def sent(copy, first_k, last_k):
        def one(k, carry):
            copy(k).wait_send()
            return carry

        pending.append(lambda: lax.fori_loop(first_k, last_k, one, 0))

    barrier = pltpu.get_barrier_semaphore()

    def greet(device):
        pl.semaphore_signal(barrier, inc=1, device_id=device, device_id_type=MESH)

    def greetings():
        for k in range(1, 4):
            greet(first(k))
            greet(second(k))
        for k in range(1, 8):
            greet(on_slide(k // 2, k % 2))

    pairs = (
        (tiles_h, tiles), (mlp_gain_h, mlp_gain), (mlp_bias_h, mlp_bias),
        (gate_h, gate), (up_h, up), (down_h, down), (slot_h, slot), (layer_scale_h, layer_scale),
        (final_gain_h, final_gain), (final_bias_h, final_bias), (patch_h, patch), (patch_bias_h, patch_bias),
        (wk_h, wk), (wv_h, wv), (wq_h, wq), (wo_h, wo), (slide_gain_h, slide_gain), (slide_bias_h, slide_bias),
        (lengths_h, lengths),
    )
    loads = [pltpu.make_async_copy(a, b, load_sem.at[i]) for i, (a, b) in enumerate(pairs)]
    for load in loads[:3]:
        load.start()
    greetings()
    for load in loads[3:]:
        load.start()
    for i in range(3):
        loads[i].wait()
    rows[0] = layer_norm(tiles[...], mlp_gain[...], mlp_bias[...]).astype(BF16)

    pl.semaphore_wait(barrier, 13)

    def ag1(j):
        return remote(rows.at[0], rows.at[4 * j], ag1_s.at[j], ag_r.at[4 * j], first(offset_of(j)))

    for j in range(1, 4):
        ag1(j).start()
        pending.append(ag1(j).wait_send)

    def ag2(i, j):
        return remote(
            rows.at[4 * j], rows.at[4 * j + i], ag2_s.at[4 * j + i], ag_r.at[4 * j + i], second(offset_of(i))
        )

    def spread(j):
        for i in range(1, 3):
            ag2(i, j).start()
            pending.append(ag2(i, j).wait_send)

    def far_chunk(j):
        return remote(rows.at[4 * j], rows.at[4 * j + 3], ag2_s.at[4 * j + 3], ag_r.at[4 * j + 3], second(2))

    loads[18].wait()
    length = lengths[t]
    row = iota((256, SEQ), 0)
    key = iota((256, SEQ), 1)
    head, query = row // 64, row % 64
    weight = (
        1.0
        + jnp.where((query % 2 == head % 2) & (key % 2 == head % 2), 1.0, 0.0)
        + jnp.where((query % 4 == head) & (key % 4 == head), 1.0, 0.0)
    )
    mult[...] = jnp.where(key < length, weight, 0.0)

    spread(0)
    far_chunk(0).start()
    ag1(1).wait_recv()
    spread(1)
    far_chunk(1).start()
    ag1(2).wait_recv()
    spread(2)
    far_chunk(2).start()
    ag1(3).wait_recv()
    far_chunk(3).start()
    spread(3)
    pending.append(far_chunk(0).wait_send)
    pending.append(far_chunk(1).wait_send)
    pending.append(far_chunk(2).wait_send)
    pending.append(far_chunk(3).wait_send)
    for i in range(3, 6):
        loads[i].wait()

    def rs1(i, j):
        return remote(
            part.at[4 * j + i], got1.at[j, i - 1], rs1_s.at[4 * j + i], rs1_r.at[4 * j + i], second(4 - offset_of(i))
        )

    def batch(j, carry):
        ag2(1, j).wait_recv()
        ag2(2, j).wait_recv()
        far_chunk(j).wait_recv()

        block = rows[pl.ds(4 * j, 4)].reshape(128, D_TILE)
        gate_out = jnp.dot(block, gate[...], preferred_element_type=F32)
        up_out = jnp.dot(block, up[...], preferred_element_type=F32)
        hidden = (gate_out / (1.0 + jnp.exp(-gate_out)) * up_out).astype(BF16)
        part[pl.ds(4 * j, 4)] = (
            jnp.dot(hidden, down[...], preferred_element_type=F32).astype(BF16).reshape(4, TILE_DEV, D_TILE)
        )
        for i in (3, 1, 2):
            rs1(i, j).start()
        return carry

    lax.fori_loop(0, 4, batch, 0)
    for j in range(4):
        for i in range(1, 4):
            pending.append(rs1(i, j).wait_send)

    loads[6].wait()
    spot = slot[...]
    row_id = iota((128, TILE_DEV), 0)
    match = (spot // 512 == row_id // 8) & ((spot // 64) % 8 == row_id % 8)
    place = jnp.sum(jnp.where(match, (spot % 512 + 1).astype(F32), 0.0), axis=1, keepdims=True)
    pos_out[...] = jnp.broadcast_to(place, (128, 128)).reshape(16, 8, 128)
    pos_in[0] = pos_out[t]

    def pos_copy(k):
        return remote(pos_out.at[on_tile(k)[1]], pos_in.at[k], pos_s.at[k], pos_r.at[k], on_tile(k))

    def pos_start(k, carry):
        pos_copy(k).start()
        return carry

    lax.fori_loop(1, 16, pos_start, 0)
    sent(pos_copy, 1, 16)

    for i in range(12, 16):
        loads[i].wait()

    def convert(k, carry):
        at = pl.ds(pl.multiple_of(k * 128, 128), 128)
        wkv16[at, 0:D_SLIDE] = wk[at, :].astype(BF16)
        wkv16[at, D_SLIDE : 2 * D_SLIDE] = wv[at, :].astype(BF16)
        wq16[at, :] = wq[at, :].astype(BF16)
        wo16[at, :] = wo[at, :].astype(BF16)
        return carry

    lax.fori_loop(0, 6, convert, 0)

    def rs2(j):
        return remote(fold.at[j - 1], got2.at[j - 1], rs2_s.at[j], rs2_r.at[j], first(4 - offset_of(j)))

    def line_sum(j):
        for i in range(1, 4):
            rs1(i, j).wait_recv()
        return (
            part[4 * j].astype(F32) + got1[j, 0].astype(F32) + got1[j, 1].astype(F32) + got1[j, 2].astype(F32)
        )

    for j in range(1, 4):
        fold[j - 1] = line_sum(j).astype(BF16)
        rs2(j).start()
        pending.append(rs2(j).wait_send)
    mixed = line_sum(0)

    def pos_wait(k, carry):
        pos_copy(k).wait_recv()
        return carry

    lax.fori_loop(1, 16, pos_wait, 0)
    turned = jnp.transpose(pos_in[...].reshape(128, 128))
    pos_all[0] = turned[0:8]

    def pa_copy(k):
        return remote(pos_all.at[0], pos_all.at[k], pa_s.at[k], pa_r.at[k], on_slide(k // 2, k % 2))

    def pa_start(k, carry):
        pa_copy(k).start()
        return carry

    lax.fori_loop(1, 8, pa_start, 0)
    sent(pa_copy, 1, 8)

    for i in range(7, 12):
        loads[i].wait()
    for j in range(1, 4):
        rs2(j).wait_recv()
    mixed = mixed + got2[0].astype(F32) + got2[1].astype(F32) + got2[2].astype(F32)
    final = layer_norm(tiles[...] + layer_scale[...] * mixed, final_gain[...], final_bias[...]).astype(BF16)
    embed = (jnp.dot(final, patch[...], preferred_element_type=F32) + patch_bias[...]).astype(BF16)

    slot_id = iota((256, TILE_DEV), 0)
    hit = (spot // 512 == slot_id // 16) & ((spot // 64) % 8 == slot_id % 8)
    left = jnp.where(hit & (slot_id % 16 < 8), 1.0, 0.0).astype(BF16)
    right = jnp.where(hit & (slot_id % 16 >= 8), 1.0, 0.0).astype(BF16)
    send_slots[...] = (
        (
            jnp.dot(left, embed[:, 0:384], preferred_element_type=F32)
            + jnp.dot(right, embed[:, 384:768], preferred_element_type=F32)
        )
        .astype(BF16)
        .reshape(16, 16, 384)
    )

    def slot_copy(k):
        return remote(send_slots.at[on_tile(k)[1]], got_slots.at[k], sl_s.at[k], sl_r.at[k], on_tile(k))

    def slot_start(k, carry):
        slot_copy(k).start()
        return carry

    lax.fori_loop(1, 16, slot_start, 0)
    drain()
    sent(slot_copy, 1, 16)
    got_slots[0] = send_slots[t]

    def pa_wait(k, carry):
        pa_copy(k).wait_recv()
        return carry

    lax.fori_loop(1, 8, pa_wait, 0)
    position = (iota((SEQ, 128), 0) + 1).astype(F32)
    for k in range(8):
        one_hot[:, k * 128 : (k + 1) * 128] = jnp.where(position == pos_all[k][0:1], 1.0, 0.0).astype(BF16)

    def along(e, q, dx):
        return remote(slots.at[0, q], slots.at[e, q], dg_s.at[4 * e + q], dg_r.at[4 * e + q], on_slide(dx, 0))

    def near(e, q):
        at = 4 * e + 4 + q
        return remote(slots.at[e, q], slots.at[e + 1, q], dg_s.at[at], dg_r.at[at], on_slide(0, 1))

    order = (0, 1, 3, 2)
    for q in order:
        for k in range(4 * q, 4 * q + 4):
            if k > 0:
                slot_copy(k).wait_recv()
        wide = got_slots[4 * q : 4 * q + 4].astype(F32)
        slots[0, q, :, 0:384] = wide[:, 0:8, :].reshape(32, 384).astype(BF16)
        slots[0, q, :, 384:768] = wide[:, 8:16, :].reshape(32, 384).astype(BF16)
        along(4, q, 2).start()
        pending.append(along(4, q, 2).wait_send)
        along(2, q, 1).start()
        along(6, q, 3).start()
        near(0, q).start()
        pending.append(along(2, q, 1).wait_send)
        pending.append(along(6, q, 3).wait_send)
        pending.append(near(0, q).wait_send)

    def came(e, q):
        along(e, q, 0).wait_recv()
        near(e, q).start()
        pending.append(near(e, q).wait_send)

    def place_pair(k):
        return jnp.dot(
            one_hot[:, k * 128 : (k + 2) * 128], slots[k : k + 2].reshape(256, D_SLIDE), preferred_element_type=F32
        )

    def arrive(q):
        for e in (2 + 4 * c, 6 - 4 * c, 4):
            came(e, q)

    drain()
    for q in order[:3]:
        arrive(q)
    for q in order:
        near(0, q).wait_recv()
    canvas[...] = place_pair(0)
    arrive(order[3])
    for k in (2, 6, 4):
        for q in order:
            near(k, q).wait_recv()
        canvas[...] += place_pair(k)
    for i in range(16, 18):
        loads[i].wait()
    normed_all[...] = layer_norm(canvas[...], slide_gain[...], slide_bias[...]).astype(BF16)
    mine = pl.ds(pl.multiple_of(s * SEQ_DEV, SEQ_DEV), SEQ_DEV)
    kv[...] = jnp.dot(normed_all[...], wkv16[...], preferred_element_type=F32).astype(BF16)
    queries = jnp.dot(normed_all[mine, :], wq16[...], preferred_element_type=F32) * HEAD_DIM ** (-0.5)

    head_row = iota((256, 256), 0) // 64
    lane = iota((256, 256), 1)
    att[...] = jnp.zeros_like(att)
    for w, start in enumerate((0, 128, 384, 512)):
        low = (4 * w + head_row) * HEAD_DIM - start
        own = (lane >= low) & (lane < low + HEAD_DIM)
        window = queries[:, start : start + 256]
        stacked = jnp.where(own, jnp.concatenate([window] * 4, axis=0), 0.0).astype(BF16)
        scores = lax.dot_general(
            stacked, kv[:, start : start + 256], (((1,), (1,)), ((), ())), preferred_element_type=F32
        )
        counted = mult[...]
        scores = jnp.where(counted > 0.0, scores, masked_score)
        weights = jnp.exp(scores - jnp.max(scores, axis=1, keepdims=True)) * counted
        total = jnp.sum(weights, axis=1, keepdims=True)
        mixed_rows = jnp.dot(
            weights.astype(BF16), kv[:, D_SLIDE + start : D_SLIDE + start + 256], preferred_element_type=F32
        )
        mixed_rows = jnp.where(own, mixed_rows / total, 0.0)
        att[:, start : start + 256] += (
            mixed_rows[0:64] + mixed_rows[64:128] + mixed_rows[128:192] + mixed_rows[192:256]
        )
    result = canvas[mine, :] + jnp.dot(att[...].astype(BF16), wo16[...], preferred_element_type=F32)
    here = iota((SEQ_DEV, D_SLIDE), 0) + s * SEQ_DEV
    out[0] = jnp.where(here < length, result, 0.0)

    drain()


def per_device(
    tiles, mlp_gain, mlp_bias, gate_weight, up_weight, down_weight, layer_scale, final_gain, final_bias,
    patch_weight, patch_bias, slide_gain, slide_bias, w_query, w_key, w_value, w_out, slide_lengths, tile_slot,
):
    hbm = pl.BlockSpec(memory_space=pl.ANY)
    dma = pltpu.SemaphoreType.DMA
    vm = pltpu.VMEM
    return pl.pallas_call(
        kernel,
        out_shape=pltpu.VMEM((1, SEQ_DEV, D_SLIDE), F32),
        in_specs=[hbm] * 19,
        out_specs=pl.BlockSpec(memory_space=pltpu.VMEM),
        scratch_shapes=[
            vm((TILE_DEV, D_TILE), F32), vm((D_TILE,), F32), vm((D_TILE,), F32),
            vm((D_TILE, GROUP), BF16), vm((D_TILE, GROUP), BF16), vm((GROUP, D_TILE), BF16),
            vm((D_TILE,), F32), vm((D_TILE,), F32), vm((D_TILE,), F32),
            vm((D_TILE, D_SLIDE), BF16), vm((D_SLIDE,), F32), vm((D_SLIDE,), F32), vm((D_SLIDE,), F32),
            vm((D_SLIDE, D_SLIDE), F32), vm((D_SLIDE, D_SLIDE), F32),
            vm((D_SLIDE, D_SLIDE), F32), vm((D_SLIDE, D_SLIDE), F32),
            vm((1, TILE_DEV), jnp.int32), pltpu.SMEM((16,), jnp.int32),
            vm((16, TILE_DEV, D_TILE), BF16), vm((16, TILE_DEV, D_TILE), BF16),
            vm((4, 3, TILE_DEV, D_TILE), BF16), vm((3, TILE_DEV, D_TILE), BF16), vm((3, TILE_DEV, D_TILE), BF16),
            vm((D_SLIDE, 2 * D_SLIDE), BF16), vm((D_SLIDE, D_SLIDE), BF16), vm((D_SLIDE, D_SLIDE), BF16),
            vm((16, 8, 128), F32), vm((16, 8, 128), F32), vm((8, 8, 128), F32),
            vm((16, 16, 384), BF16), vm((16, 16, 384), BF16), vm((8, 4, 32, D_SLIDE), BF16),
            vm((SEQ, 1024), BF16), vm((SEQ, D_SLIDE), F32), vm((SEQ, D_SLIDE), BF16),
            vm((SEQ, 2 * D_SLIDE), BF16), vm((256, SEQ), F32), vm((SEQ_DEV, D_SLIDE), F32),
            dma((19,)), dma((4,)), dma((16,)), dma((16,)), dma((16,)), dma((16,)), dma((4,)), dma((4,)),
            dma((16,)), dma((16,)), dma((8,)), dma((8,)), dma((16,)), dma((16,)), dma((32,)), dma((32,)),
        ],
        compiler_params=pltpu.CompilerParams(
            collective_id=0, has_side_effects=True, vmem_limit_bytes=56 * 2**20
        ),
        name="slide_kernel",
    )(
        tiles, mlp_gain, mlp_bias, gate_weight, up_weight, down_weight, layer_scale,
        final_gain, final_bias, patch_weight, patch_bias, slide_gain, slide_bias,
        w_query, w_key, w_value, w_out, slide_lengths, tile_slot.reshape(1, TILE_DEV),
    )


def solution(mesh):
    both = P(("slide", "tile"))
    placed = (
        P(("slide", "tile"), None), P(), P(), P(None, "tile"), P(None, "tile"), P("tile", None),
        P(), P(), P(), P(), P(), P(), P(), P(), P(), P(), P(), P(), both,
    )
    return jax.shard_map(
        per_device, mesh=mesh, in_specs=placed, out_specs=P("tile", "slide", None), check_vma=False
    )
```

```python
import jax
import jax.numpy as jnp
from jax import lax
from jax.experimental import pallas as pl
from jax.experimental.pallas import tpu as pltpu
from jax.sharding import PartitionSpec as P

D_TILE = 1536
D_SLIDE = 768
HEADS = 16
HEAD_DIM = 48
TILE_DEV = 32
SEQ_DEV = 64
SEQ = 512
GROUP = 256
MESH = pl.DeviceIdType.MESH
F32 = jnp.float32
BF16 = jnp.bfloat16
epsilon = 1e-06
masked_score = -1e30


def layer_norm(values, scale_vec, shift_vec):
    average = jnp.mean(values, axis=-1, keepdims=True)
    centred = values - average
    variance = jnp.mean(centred * centred, axis=-1, keepdims=True)
    return centred * lax.rsqrt(variance + epsilon) * scale_vec + shift_vec


def iota(shape, dim):
    return lax.broadcasted_iota(jnp.int32, shape, dim)


def offset_of(i):
    return i + (i // 2) * (1 - 2 * (i % 2))


def kernel(
    tiles_h, mlp_gain_h, mlp_bias_h, gate_h, up_h, down_h, layer_scale_h, final_gain_h, final_bias_h,
    patch_h, patch_bias_h, slide_gain_h, slide_bias_h, wq_h, wk_h, wv_h, wo_h, lengths_h, slot_h,
    out,
    tiles, mlp_gain, mlp_bias, gate, up, down, layer_scale, final_gain, final_bias,
    patch, patch_bias, slide_gain, slide_bias, wq, wk, wv, wo, slot, lengths,
    rows, part, got1, fold, got2, wkv16, wq16, wo16,
    pos_out, pos_in, pos_all, send_slots, got_slots, slots, one_hot, canvas, normed_all, kv, mult, att,
    load_sem, ag1_s, ag2_s, ag_r, rs1_s, rs1_r, rs2_s, rs2_r,
    pos_s, pos_r, pa_s, pa_r, sl_s, sl_r, dg_s, dg_r,
):
    s = lax.axis_index("slide")
    t = lax.axis_index("tile")
    x, c = s // 2, s % 2
    y, z = t // 4, t % 4

    def first(k):
        return (s, ((y + c * k) % 4) * 4 + (z + (1 - c) * k) % 4)

    def second(k):
        return (s, ((y + (1 - c) * k) % 4) * 4 + (z + c * k) % 4)

    def on_tile(k):
        return (s, ((y + k // 4) % 4) * 4 + (z + k) % 4)

    def on_slide(dx, dc):
        return (((x + dx) % 4) * 2 + (c + dc) % 2, t)

    def remote(src, dst, send_sem, recv_sem, device):
        return pltpu.make_async_remote_copy(
            src_ref=src, dst_ref=dst, send_sem=send_sem, recv_sem=recv_sem,
            device_id=device, device_id_type=MESH,
        )

    pending = []

    def drain():
        for wait in pending:
            wait()
        pending.clear()

    def sent(copy, first_k, last_k):
        def one(k, carry):
            copy(k).wait_send()
            return carry

        pending.append(lambda: lax.fori_loop(first_k, last_k, one, 0))

    barrier = pltpu.get_barrier_semaphore()

    def greet(device):
        pl.semaphore_signal(barrier, inc=1, device_id=device, device_id_type=MESH)

    def greetings():
        for k in range(1, 4):
            greet(first(k))
            greet(second(k))
        for k in range(1, 8):
            greet(on_slide(k // 2, k % 2))

    pairs = (
        (tiles_h, tiles), (mlp_gain_h, mlp_gain), (mlp_bias_h, mlp_bias),
        (gate_h, gate), (up_h, up), (down_h, down), (slot_h, slot), (layer_scale_h, layer_scale),
        (final_gain_h, final_gain), (final_bias_h, final_bias), (patch_h, patch), (patch_bias_h, patch_bias),
        (wk_h, wk), (wv_h, wv), (wq_h, wq), (wo_h, wo), (slide_gain_h, slide_gain), (slide_bias_h, slide_bias),
        (lengths_h, lengths),
    )
    loads = [pltpu.make_async_copy(a, b, load_sem.at[i]) for i, (a, b) in enumerate(pairs)]
    for load in loads[:3]:
        load.start()
    greetings()
    for load in loads[3:]:
        load.start()
    for i in range(3):
        loads[i].wait()
    rows[0] = layer_norm(tiles[...], mlp_gain[...], mlp_bias[...]).astype(BF16)

    pl.semaphore_wait(barrier, 13)

    def ag1(j):
        return remote(rows.at[0], rows.at[4 * j], ag1_s.at[j], ag_r.at[4 * j], first(offset_of(j)))

    for j in range(1, 4):
        ag1(j).start()
        pending.append(ag1(j).wait_send)

    def ag2(i, j):
        return remote(
            rows.at[4 * j], rows.at[4 * j + i], ag2_s.at[4 * j + i], ag_r.at[4 * j + i], second(offset_of(i))
        )

    def spread(j):
        for i in range(1, 3):
            ag2(i, j).start()
            pending.append(ag2(i, j).wait_send)

    def far_chunk(j):
        return remote(rows.at[4 * j], rows.at[4 * j + 3], ag2_s.at[4 * j + 3], ag_r.at[4 * j + 3], second(2))

    loads[18].wait()
    length = lengths[t]
    row = iota((256, SEQ), 0)
    key = iota((256, SEQ), 1)
    head, query = row // 64, row % 64
    weight = (
        1.0
        + jnp.where((query % 2 == head % 2) & (key % 2 == head % 2), 1.0, 0.0)
        + jnp.where((query % 4 == head) & (key % 4 == head), 1.0, 0.0)
    )
    mult[...] = jnp.where(key < length, weight, 0.0)

    spread(0)
    far_chunk(0).start()
    ag1(1).wait_recv()
    spread(1)
    far_chunk(1).start()
    ag1(2).wait_recv()
    spread(2)
    far_chunk(2).start()
    ag1(3).wait_recv()
    far_chunk(3).start()
    spread(3)
    pending.append(far_chunk(0).wait_send)
    pending.append(far_chunk(1).wait_send)
    pending.append(far_chunk(2).wait_send)
    pending.append(far_chunk(3).wait_send)
    for i in range(3, 6):
        loads[i].wait()

    def rs1(i, j):
        return remote(
            part.at[4 * j + i], got1.at[j, i - 1], rs1_s.at[4 * j + i], rs1_r.at[4 * j + i], second(4 - offset_of(i))
        )

    def batch(j, carry):
        ag2(1, j).wait_recv()
        ag2(2, j).wait_recv()
        far_chunk(j).wait_recv()

        block = rows[pl.ds(4 * j, 4)].reshape(128, D_TILE)
        gate_out = jnp.dot(block, gate[...], preferred_element_type=F32)
        up_out = jnp.dot(block, up[...], preferred_element_type=F32)
        hidden = (gate_out / (1.0 + jnp.exp(-gate_out)) * up_out).astype(BF16)
        part[pl.ds(4 * j, 4)] = (
            jnp.dot(hidden, down[...], preferred_element_type=F32).astype(BF16).reshape(4, TILE_DEV, D_TILE)
        )
        for i in (3, 1, 2):
            rs1(i, j).start()
        return carry

    lax.fori_loop(0, 4, batch, 0)
    for j in range(4):
        for i in range(1, 4):
            pending.append(rs1(i, j).wait_send)

    loads[6].wait()
    spot = slot[...]
    row_id = iota((128, TILE_DEV), 0)
    match = (spot // 512 == row_id // 8) & ((spot // 64) % 8 == row_id % 8)
    place = jnp.sum(jnp.where(match, (spot % 512 + 1).astype(F32), 0.0), axis=1, keepdims=True)
    pos_out[...] = jnp.broadcast_to(place, (128, 128)).reshape(16, 8, 128)
    pos_in[0] = pos_out[t]

    def pos_copy(k):
        return remote(pos_out.at[on_tile(k)[1]], pos_in.at[k], pos_s.at[k], pos_r.at[k], on_tile(k))

    def pos_start(k, carry):
        pos_copy(k).start()
        return carry

    lax.fori_loop(1, 16, pos_start, 0)
    sent(pos_copy, 1, 16)

    for i in range(12, 16):
        loads[i].wait()

    def convert(k, carry):
        at = pl.ds(pl.multiple_of(k * 128, 128), 128)
        wkv16[at, 0:D_SLIDE] = wk[at, :].astype(BF16)
        wkv16[at, D_SLIDE : 2 * D_SLIDE] = wv[at, :].astype(BF16)
        wq16[at, :] = wq[at, :].astype(BF16)
        wo16[at, :] = wo[at, :].astype(BF16)
        return carry

    lax.fori_loop(0, 6, convert, 0)

    def rs2(j):
        return remote(fold.at[j - 1], got2.at[j - 1], rs2_s.at[j], rs2_r.at[j], first(4 - offset_of(j)))

    def line_sum(j):
        for i in range(1, 4):
            rs1(i, j).wait_recv()
        return (
            part[4 * j].astype(F32) + got1[j, 0].astype(F32) + got1[j, 1].astype(F32) + got1[j, 2].astype(F32)
        )

    for j in range(1, 4):
        fold[j - 1] = line_sum(j).astype(BF16)
        rs2(j).start()
        pending.append(rs2(j).wait_send)
    mixed = line_sum(0)

    def pos_wait(k, carry):
        pos_copy(k).wait_recv()
        return carry

    lax.fori_loop(1, 16, pos_wait, 0)
    turned = jnp.transpose(pos_in[...].reshape(128, 128))
    pos_all[0] = turned[0:8]

    def pa_copy(k):
        return remote(pos_all.at[0], pos_all.at[k], pa_s.at[k], pa_r.at[k], on_slide(k // 2, k % 2))

    def pa_start(k, carry):
        pa_copy(k).start()
        return carry

    lax.fori_loop(1, 8, pa_start, 0)
    sent(pa_copy, 1, 8)

    for i in range(7, 12):
        loads[i].wait()
    for j in range(1, 4):
        rs2(j).wait_recv()
    mixed = mixed + got2[0].astype(F32) + got2[1].astype(F32) + got2[2].astype(F32)
    final = layer_norm(tiles[...] + layer_scale[...] * mixed, final_gain[...], final_bias[...]).astype(BF16)
    embed = (jnp.dot(final, patch[...], preferred_element_type=F32) + patch_bias[...]).astype(BF16)

    slot_id = iota((256, TILE_DEV), 0)
    hit = (spot // 512 == slot_id // 16) & ((spot // 64) % 8 == slot_id % 8)
    left = jnp.where(hit & (slot_id % 16 < 8), 1.0, 0.0).astype(BF16)
    right = jnp.where(hit & (slot_id % 16 >= 8), 1.0, 0.0).astype(BF16)
    send_slots[...] = (
        (
            jnp.dot(left, embed[:, 0:384], preferred_element_type=F32)
            + jnp.dot(right, embed[:, 384:768], preferred_element_type=F32)
        )
        .astype(BF16)
        .reshape(16, 16, 384)
    )

    def slot_copy(k):
        return remote(send_slots.at[on_tile(k)[1]], got_slots.at[k], sl_s.at[k], sl_r.at[k], on_tile(k))

    def slot_start(k, carry):
        slot_copy(k).start()
        return carry

    lax.fori_loop(1, 16, slot_start, 0)
    drain()
    sent(slot_copy, 1, 16)
    got_slots[0] = send_slots[t]

    def pa_wait(k, carry):
        pa_copy(k).wait_recv()
        return carry

    lax.fori_loop(1, 8, pa_wait, 0)
    position = (iota((SEQ, 128), 0) + 1).astype(F32)
    for k in range(8):
        one_hot[:, k * 128 : (k + 1) * 128] = jnp.where(position == pos_all[k][0:1], 1.0, 0.0).astype(BF16)

    def along(e, q, dx):
        return remote(slots.at[0, q], slots.at[e, q], dg_s.at[4 * e + q], dg_r.at[4 * e + q], on_slide(dx, 0))

    def near(e, q):
        at = 4 * e + 4 + q
        return remote(slots.at[e, q], slots.at[e + 1, q], dg_s.at[at], dg_r.at[at], on_slide(0, 1))

    def across(e, q, dx):
        at = 4 * e + 4 + q
        return remote(slots.at[0, q], slots.at[e + 1, q], dg_s.at[at], dg_r.at[at], on_slide(dx, 1))

    order = (0, 1, 3, 2)
    for q in order:
        for k in range(4 * q, 4 * q + 4):
            if k > 0:
                slot_copy(k).wait_recv()
        wide = got_slots[4 * q : 4 * q + 4].astype(F32)
        slots[0, q, :, 0:384] = wide[:, 0:8, :].reshape(32, 384).astype(BF16)
        slots[0, q, :, 384:768] = wide[:, 8:16, :].reshape(32, 384).astype(BF16)
        along(4, q, 2).start()
        pending.append(along(4, q, 2).wait_send)
        along(2, q, 1).start()
        along(6, q, 3).start()
        near(0, q).start()
        if q == order[3]:
            for e, dx in ((4, 2), (2, 1), (6, 3)):
                across(e, q, dx).start()
                pending.append(across(e, q, dx).wait_send)
        pending.append(along(2, q, 1).wait_send)
        pending.append(along(6, q, 3).wait_send)
        pending.append(near(0, q).wait_send)

    def came(e, q):
        along(e, q, 0).wait_recv()
        if q != order[3]:
            near(e, q).start()
            pending.append(near(e, q).wait_send)

    def place_pair(k):
        return jnp.dot(
            one_hot[:, k * 128 : (k + 2) * 128], slots[k : k + 2].reshape(256, D_SLIDE), preferred_element_type=F32
        )

    def arrive(q):
        for e in (2 + 4 * c, 6 - 4 * c, 4):
            came(e, q)

    drain()
    for q in order[:3]:
        arrive(q)
    for q in order:
        near(0, q).wait_recv()
    canvas[...] = place_pair(0)
    arrive(order[3])
    for k in (2, 6, 4):
        for q in order:
            near(k, q).wait_recv()
        canvas[...] += place_pair(k)
    for i in range(16, 18):
        loads[i].wait()
    normed_all[...] = layer_norm(canvas[...], slide_gain[...], slide_bias[...]).astype(BF16)
    mine = pl.ds(pl.multiple_of(s * SEQ_DEV, SEQ_DEV), SEQ_DEV)
    kv[...] = jnp.dot(normed_all[...], wkv16[...], preferred_element_type=F32).astype(BF16)
    queries = jnp.dot(normed_all[mine, :], wq16[...], preferred_element_type=F32) * HEAD_DIM ** (-0.5)

    head_row = iota((256, 256), 0) // 64
    lane = iota((256, 256), 1)
    att[...] = jnp.zeros_like(att)
    for w, start in enumerate((0, 128, 384, 512)):
        low = (4 * w + head_row) * HEAD_DIM - start
        own = (lane >= low) & (lane < low + HEAD_DIM)
        window = queries[:, start : start + 256]
        stacked = jnp.where(own, jnp.concatenate([window] * 4, axis=0), 0.0).astype(BF16)
        scores = lax.dot_general(
            stacked, kv[:, start : start + 256], (((1,), (1,)), ((), ())), preferred_element_type=F32
        )
        counted = mult[...]
        scores = jnp.where(counted > 0.0, scores, masked_score)
        weights = jnp.exp(scores - jnp.max(scores, axis=1, keepdims=True)) * counted
        total = jnp.sum(weights, axis=1, keepdims=True)
        mixed_rows = jnp.dot(
            weights.astype(BF16), kv[:, D_SLIDE + start : D_SLIDE + start + 256], preferred_element_type=F32
        )
        mixed_rows = jnp.where(own, mixed_rows / total, 0.0)
        att[:, start : start + 256] += (
            mixed_rows[0:64] + mixed_rows[64:128] + mixed_rows[128:192] + mixed_rows[192:256]
        )
    result = canvas[mine, :] + jnp.dot(att[...].astype(BF16), wo16[...], preferred_element_type=F32)
    here = iota((SEQ_DEV, D_SLIDE), 0) + s * SEQ_DEV
    out[0] = jnp.where(here < length, result, 0.0)

    drain()


def per_device(
    tiles, mlp_gain, mlp_bias, gate_weight, up_weight, down_weight, layer_scale, final_gain, final_bias,
    patch_weight, patch_bias, slide_gain, slide_bias, w_query, w_key, w_value, w_out, slide_lengths, tile_slot,
):
    hbm = pl.BlockSpec(memory_space=pl.ANY)
    dma = pltpu.SemaphoreType.DMA
    vm = pltpu.VMEM
    return pl.pallas_call(
        kernel,
        out_shape=pltpu.VMEM((1, SEQ_DEV, D_SLIDE), F32),
        in_specs=[hbm] * 19,
        out_specs=pl.BlockSpec(memory_space=pltpu.VMEM),
        scratch_shapes=[
            vm((TILE_DEV, D_TILE), F32), vm((D_TILE,), F32), vm((D_TILE,), F32),
            vm((D_TILE, GROUP), BF16), vm((D_TILE, GROUP), BF16), vm((GROUP, D_TILE), BF16),
            vm((D_TILE,), F32), vm((D_TILE,), F32), vm((D_TILE,), F32),
            vm((D_TILE, D_SLIDE), BF16), vm((D_SLIDE,), F32), vm((D_SLIDE,), F32), vm((D_SLIDE,), F32),
            vm((D_SLIDE, D_SLIDE), F32), vm((D_SLIDE, D_SLIDE), F32),
            vm((D_SLIDE, D_SLIDE), F32), vm((D_SLIDE, D_SLIDE), F32),
            vm((1, TILE_DEV), jnp.int32), pltpu.SMEM((16,), jnp.int32),
            vm((16, TILE_DEV, D_TILE), BF16), vm((16, TILE_DEV, D_TILE), BF16),
            vm((4, 3, TILE_DEV, D_TILE), BF16), vm((3, TILE_DEV, D_TILE), BF16), vm((3, TILE_DEV, D_TILE), BF16),
            vm((D_SLIDE, 2 * D_SLIDE), BF16), vm((D_SLIDE, D_SLIDE), BF16), vm((D_SLIDE, D_SLIDE), BF16),
            vm((16, 8, 128), F32), vm((16, 8, 128), F32), vm((8, 8, 128), F32),
            vm((16, 16, 384), BF16), vm((16, 16, 384), BF16), vm((8, 4, 32, D_SLIDE), BF16),
            vm((SEQ, 1024), BF16), vm((SEQ, D_SLIDE), F32), vm((SEQ, D_SLIDE), BF16),
            vm((SEQ, 2 * D_SLIDE), BF16), vm((256, SEQ), F32), vm((SEQ_DEV, D_SLIDE), F32),
            dma((19,)), dma((4,)), dma((16,)), dma((16,)), dma((16,)), dma((16,)), dma((4,)), dma((4,)),
            dma((16,)), dma((16,)), dma((8,)), dma((8,)), dma((16,)), dma((16,)), dma((32,)), dma((32,)),
        ],
        compiler_params=pltpu.CompilerParams(
            collective_id=0, has_side_effects=True, vmem_limit_bytes=56 * 2**20
        ),
        name="slide_kernel",
    )(
        tiles, mlp_gain, mlp_bias, gate_weight, up_weight, down_weight, layer_scale,
        final_gain, final_bias, patch_weight, patch_bias, slide_gain, slide_bias,
        w_query, w_key, w_value, w_out, slide_lengths, tile_slot.reshape(1, TILE_DEV),
    )


def solution(mesh):
    both = P(("slide", "tile"))
    placed = (
        P(("slide", "tile"), None), P(), P(), P(None, "tile"), P(None, "tile"), P("tile", None),
        P(), P(), P(), P(), P(), P(), P(), P(), P(), P(), P(), P(), both,
    )
    return jax.shard_map(
        per_device, mesh=mesh, in_specs=placed, out_specs=P("tile", "slide", None), check_vma=False
    )
```
